32 devices in a mesh: tm: 4 (over y, core), rows: 8 (over z, x).
Axes of the slice: x: 2, y: 2, z: 4, core: 2. Of those that a mesh axis runs over, the one named last changes fastest.
Arguments:
- latent: bfloat16 [8, 32, 16, 384], P('tm', 'rows'), may hold values from -6 to 6
- gain_first: float32 [384], replicated, may hold values from 0.5 to 2
- conv_first: bfloat16 [27, 384, 384], P(None, 'tm'), may hold values from -0.0625 to 0.0625
- bias_first: float32 [384], replicated, may hold values from -0.5 to 0.5
- conv_upper: bfloat16 [9, 384, 192], replicated, may hold values from -0.109375 to 0.109375
- bias_upper: float32 [192], replicated, may hold values from -0.5 to 0.5
Outputs:
- decoded: bfloat16 [8, 64, 6144], P('tm', 'rows')
The draws below stay inside these ranges and needn't reach their ends.
All inputs are finite; a program needn't handle non-finite values.
Results may differ from the reference program's by a relative error of at most 0.0052.
Values may be sent and summed in bfloat16 or wider, within the bound.
A program may use at most 64 MiB of HBM per device.

```python
import math
import jax
import jax.numpy as jnp
from jax import lax

C = 384
CO = 192
W = 16
NT = 8
NH = 32


def level_of(key, shape, split, smallest, high):
    def one(axis_at, parts):
        draws = jax.random.uniform(jax.random.fold_in(jax.random.fold_in(key, 6), axis_at), (parts,), jnp.float32, smallest / len(split), high / len(split))
        return jnp.repeat(jnp.exp(draws), shape[axis_at] // parts).reshape((-1,) + (1,) * (len(shape) - axis_at - 1))

    level = one(*split[0])
    for cut in split[1:]:
        level = level * one(*cut)
    return level


def scatter_about(key, dims, scale, most, split=(), kind=jnp.bfloat16):
    loudness = level_of(key, dims, split, -0.22, 0.18) if split else 1.0
    values = jax.random.normal(key, dims, jnp.float32) * scale * loudness
    return jnp.minimum(jnp.maximum(values, -most), most).astype(kind)


def setup_inputs(seed: int = 0) -> dict:
    key_list = jax.random.split(jax.random.key(seed), 7)
    latent = scatter_about(key_list[0], (NT, NH, W, C), 1.0, 6.0, ((0, 4), (1, 8)))
    gain_first = jnp.clip(jnp.exp(jax.random.uniform(key_list[1], (C,), jnp.float32, math.log(0.5), math.log(2.0))), 0.5, 2.0)
    conv_first = scatter_about(key_list[2], (27, C, C), (27 * C) ** -0.5, 0.0625, ((1, 4),))
    bias_first = jnp.clip(jax.random.uniform(key_list[3], (C,), jnp.float32, -0.5, 0.5), -0.5, 0.5)
    conv_upper = scatter_about(key_list[4], (9, C, CO), (9 * C) ** -0.5, 0.109375)
    bias_upper = jnp.clip(jax.random.uniform(key_list[5], (CO,), jnp.float32, -0.5, 0.5), -0.5, 0.5)
    return {"latent": latent, "gain_first": gain_first, "conv_first": conv_first, "bias_first": bias_first, "conv_upper": conv_upper, "bias_upper": bias_upper}


def scaled_silu(features, gain):
    values = features.astype(jnp.float32)
    mean_square = lax.optimization_barrier(jnp.mean(values * values, axis=-1, keepdims=True))
    scaled = values * lax.rsqrt(mean_square + 1e-06) * gain.astype(jnp.float32)
    return (scaled * jax.nn.sigmoid(scaled)).astype(jnp.bfloat16)

def causal_conv(activated, kernel, bias):
    chans = activated.shape[-1]
    values = activated.astype(jnp.float32)
    padded = jnp.pad(values, ((2, 0), (1, 1), (1, 1), (0, 0)))
    weights = kernel.astype(jnp.float32).reshape(3, 3, 3, chans, kernel.shape[-1])
    result = lax.conv_general_dilated(padded[None], weights, (1, 1, 1), 'VALID', dimension_numbers=('NDHWC', 'DHWIO', 'NDHWC'), precision=lax.Precision.HIGHEST)[0]
    return result + bias.astype(jnp.float32)

def reference(latent, gain_first, conv_first, bias_first, conv_upper, bias_upper):
    first_act = scaled_silu(latent, gain_first)
    conv_out = causal_conv(first_act, conv_first, bias_first)
    block_out = (latent.astype(jnp.float32) + conv_out).astype(jnp.bfloat16)
    chans = conv_upper.shape[1]
    outputs = conv_upper.shape[2]
    upper_weights = conv_upper.astype(jnp.float32).reshape(3, 3, chans, outputs)

    def one_frame(frame):
        values = frame.astype(jnp.float32)
        larger = jnp.repeat(jnp.repeat(values, 2, axis=0), 2, axis=1)
        result = lax.conv_general_dilated(larger[None], upper_weights, (1, 1), ((1, 1), (1, 1)), dimension_numbers=('NHWC', 'HWIO', 'NHWC'), precision=lax.Precision.HIGHEST)[0]
        result = (result + bias_upper.astype(jnp.float32)).astype(jnp.bfloat16)
        return result.reshape(result.shape[0], result.shape[1] * result.shape[2])
    return lax.map(one_frame, block_out)
```

```python
import functools

import jax
import jax.numpy as jnp
from jax import lax
from jax.experimental import pallas as pl
from jax.experimental.pallas import tpu as pltpu
from jax.sharding import PartitionSpec as P

MESH = pl.DeviceIdType.MESH
F32 = jnp.float32
BF16 = jnp.bfloat16
LANES = 128


def kernel(
    n_tm,
    n_rows,
    latent_ref,
    small_ref,
    w1_hbm,
    wu_hbm,
    out_ref,
    w1_ref,
    wpad,
    wu_ref,
    send,
    recv,
    shifted,
    part_send,
    part_recv,
    own,
    block,
    pick,
    load_sem,
    act_send_sem,
    act_recv_sem,
    part_send_sem,
    part_recv_sem,
    row_send_sem,
    row_recv_sem,
):
    frames, rows, width, chans = latent_ref.shape
    cells = frames * rows * width
    taps, piece, _ = w1_ref.shape
    outputs = wu_ref.shape[1]
    me = lax.axis_index("tm")
    band = lax.axis_index("rows")
    above = lax.rem(band + n_rows - 1, n_rows)
    below = lax.rem(band + 1, n_rows)
    has_above = band > 0
    has_below = band < n_rows - 1

    load_w1 = pltpu.make_async_copy(w1_hbm, w1_ref, load_sem.at[0])
    load_w1.start()
    load_wu = pltpu.make_async_copy(wu_hbm, wu_ref, load_sem.at[1])
    load_wu.start()

    barrier = pltpu.get_barrier_semaphore()
    for d in range(1, n_tm):
        pl.semaphore_signal(
            barrier, inc=1, device_id=(lax.rem(me + d, n_tm), band), device_id_type=MESH
        )

    @pl.when(has_above)
    def _():
        for s in range(n_tm):
            pl.semaphore_signal(barrier, inc=1, device_id=(s, above), device_id_type=MESH)

    @pl.when(has_below)
    def _():
        for s in range(n_tm):
            pl.semaphore_signal(barrier, inc=1, device_id=(s, below), device_id_type=MESH)

    values = latent_ref[...].astype(F32).reshape(cells, chans)
    mean_square = jnp.mean(values * values, axis=-1, keepdims=True)
    scaled = values * lax.rsqrt(mean_square + 1e-06) * small_ref[pl.ds(0, 1)]
    act = scaled / (1.0 + jnp.exp(-scaled))
    blank = jnp.zeros((cells, LANES - piece), F32)
    for s in range(n_tm):
        cut = jnp.concatenate([act[:, s * piece : (s + 1) * piece], blank], axis=1)
        send[s] = cut.astype(BF16).reshape(frames, rows, width, LANES)

    neighbours = jnp.where(has_above, n_tm, 0) + jnp.where(has_below, n_tm, 0)
    pl.semaphore_wait(barrier, n_tm - 1 + neighbours)

    mine = pl.ds(me * frames, frames)

    def act_copy(s, kind, row, where, to):
        return pltpu.make_async_remote_copy(
            src_ref=send.at[s, :, row],
            dst_ref=recv.at[mine, where],
            send_sem=act_send_sem.at[3 * s + kind],
            recv_sem=act_recv_sem.at[3 * me + kind],
            device_id=(s, to),
            device_id_type=MESH,
        )

    def main_copy(s):
        return act_copy(s, 0, pl.ds(0, rows), pl.ds(1, rows), band)

    def down_copy(s):
        return act_copy(s, 1, pl.ds(rows - 1, 1), pl.ds(0, 1), below)

    def up_copy(s):
        return act_copy(s, 2, pl.ds(0, 1), pl.ds(rows + 1, 1), above)

    for d in range(1, n_tm):
        main_copy(lax.rem(me + d, n_tm)).start()

    @pl.when(has_below)
    def _():
        for s in range(n_tm):
            down_copy(s).start()

    @pl.when(has_above)
    def _():
        for s in range(n_tm):
            up_copy(s).start()

    recv[mine, pl.ds(1, rows)] = send[me]
    all_frames = n_tm * frames
    edge = jnp.zeros((all_frames, 1, width, LANES), BF16)
    block_edge = jnp.zeros((frames, 1, width, chans), BF16)

    @pl.when(band == 0)
    def _():
        recv[:, pl.ds(0, 1)] = edge
        block[:, pl.ds(0, 1)] = block_edge

    @pl.when(band == n_rows - 1)
    def _():
        recv[:, pl.ds(rows + 1, 1)] = edge
        block[:, pl.ds(rows + 1, 1)] = block_edge

    shifted[:, pl.ds(0, 2)] = jnp.zeros((3, 2, rows + 2, width, LANES), BF16)

    big = 2 * rows
    depth = block.shape[1]
    block[:, pl.ds(rows + 2, depth - rows - 2)] = jnp.zeros(
        (frames, depth - rows - 2, width, chans), BF16
    )
    at = lax.broadcasted_iota(jnp.int32, (pick.shape[0], 1), 0)
    to = lax.broadcasted_iota(jnp.int32, pick.shape, 1)
    row_tap = at // (frames * width * big)
    col = (at // (frames * big)) % width
    frame = (at // big) % frames
    line = at % big
    source = frame * (depth * width) + ((line + row_tap + 1) // 2) * width + col
    pick[...] = jnp.where(to == source, 1.0, 0.0).astype(BF16)

    load_w1.wait()
    spare = jnp.zeros((LANES - piece, chans), BF16)
    for tap in range(taps):
        wpad[pl.ds(tap * LANES, LANES)] = jnp.concatenate([w1_ref[tap], spare], axis=0)

    def act_arrival(s, kind, row, where):
        return pltpu.make_async_remote_copy(
            src_ref=send.at[s, :, row],
            dst_ref=recv.at[pl.ds(s * frames, frames), where],
            send_sem=act_send_sem.at[3 * s + kind],
            recv_sem=act_recv_sem.at[3 * s + kind],
            device_id=(lax.rem(me + 1, n_tm), band),
            device_id_type=MESH,
        )

    for d in range(1, n_tm):
        s = lax.rem(me + d, n_tm)
        act_arrival(s, 0, pl.ds(0, rows), pl.ds(1, rows)).wait_recv()

    @pl.when(has_above)
    def _():
        for s in range(n_tm):
            act_arrival(s, 1, pl.ds(0, 1), pl.ds(0, 1)).wait_recv()

    @pl.when(has_below)
    def _():
        for s in range(n_tm):
            act_arrival(s, 2, pl.ds(0, 1), pl.ds(rows + 1, 1)).wait_recv()

    tall = all_frames * (rows + 2) * width
    flat = recv[...].astype(F32).reshape(tall, LANES)
    column = lax.broadcasted_iota(jnp.int32, (tall, LANES), 0) % width
    left = jnp.where(column == 0, 0.0, pltpu.roll(flat, 1, 0))
    right = jnp.where(column == width - 1, 0.0, pltpu.roll(flat, tall - 1, 0))
    shape = (all_frames, rows + 2, width, LANES)
    shifted[0, pl.ds(2, all_frames)] = left.astype(BF16).reshape(shape)
    shifted[1, pl.ds(2, all_frames)] = recv[...]
    shifted[2, pl.ds(2, all_frames)] = right.astype(BF16).reshape(shape)

    pairs = n_tm // 2

    def part_copy(s):
        return pltpu.make_async_remote_copy(
            src_ref=part_send.at[s],
            dst_ref=part_recv.at[me],
            send_sem=part_send_sem.at[s],
            recv_sem=part_recv_sem.at[me],
            device_id=(s, band),
            device_id_type=MESH,
        )

    for k in range(1, pairs + 1):
        pair = lax.rem(lax.div(me, 2) + k, pairs)
        total = jnp.zeros((2 * cells, chans), F32)
        for dt in range(3):
            windows = []
            for dy in range(3):
                for dx in range(3):
                    start = pair * (2 * frames) + dt
                    view = shifted[dx, pl.ds(start, 2 * frames), pl.ds(dy, rows)]
                    windows.append(view.reshape(2 * cells, LANES))
            total = total + jnp.dot(
                jnp.concatenate(windows, axis=1),
                wpad[pl.ds(dt * 9 * LANES, 9 * LANES)],
                preferred_element_type=F32,
            )
        if k < pairs:
            for c in range(2):
                part_send[2 * pair + c] = total[c * cells : (c + 1) * cells].astype(BF16)
                part_copy(2 * pair + c).start()
        else:
            own[...] = total.reshape(2, cells, chans)
            mate = 2 * lax.div(me, 2) + (1 - lax.rem(me, 2))
            part_send[mate] = own[1 - lax.rem(me, 2)].astype(BF16)
            part_copy(mate).start()

    summed = own[lax.rem(me, 2)] + small_ref[pl.ds(8, 1)]
    summed = summed + latent_ref[...].astype(F32).reshape(cells, chans)
    for d in range(1, n_tm):
        s = lax.rem(me + n_tm - d, n_tm)
        pltpu.make_async_remote_copy(
            src_ref=part_send.at[s],
            dst_ref=part_recv.at[s],
            send_sem=part_send_sem.at[s],
            recv_sem=part_recv_sem.at[s],
            device_id=(s, band),
            device_id_type=MESH,
        ).wait_recv()
        summed = summed + part_recv[s].astype(F32)
    block[:, pl.ds(1, rows)] = summed.astype(BF16).reshape(frames, rows, width, chans)

    def row_copy(kind, row, where, to):
        return pltpu.make_async_remote_copy(
            src_ref=block.at[:, pl.ds(row, 1)],
            dst_ref=block.at[:, pl.ds(where, 1)],
            send_sem=row_send_sem.at[kind],
            recv_sem=row_recv_sem.at[kind],
            device_id=(me, to),
            device_id_type=MESH,
        )

    @pl.when(has_below)
    def _():
        row_copy(0, rows, 0, below).start()

    @pl.when(has_above)
    def _():
        row_copy(1, 1, rows + 1, above).start()

    load_wu.wait()

    @pl.when(has_above)
    def _():
        row_copy(0, rows, 0, above).wait_recv()

    @pl.when(has_below)
    def _():
        row_copy(1, 1, rows + 1, below).wait_recv()

    spread = jnp.dot(
        pick[...],
        block[...].reshape(frames * depth * width, chans),
        preferred_element_type=F32,
    ).astype(BF16)
    high = frames * width * big
    lines = jnp.concatenate([spread[k * high : (k + 1) * high] for k in range(3)], axis=1)
    cols = []
    for dx in range(3):
        weights = jnp.concatenate([wu_ref[dx], wu_ref[3 + dx], wu_ref[6 + dx]], axis=1)
        product = lax.dot_general(
            lines, weights, (((1,), (1,)), ((), ())), preferred_element_type=F32
        )
        cols.append(product.reshape(width, frames * big, outputs))
    nothing = jnp.zeros((1, frames * big, outputs), F32)
    before = jnp.concatenate([nothing, cols[0][: width - 1]], axis=0)
    after = jnp.concatenate([cols[2][1:], nothing], axis=0)
    bias2 = small_ref[pl.ds(16, 1)].reshape(1, 1, 2 * outputs)
    even = before + cols[1] + cols[2]
    odd = cols[0] + cols[1] + after
    both = (jnp.concatenate([even, odd], axis=-1) + bias2).astype(BF16)
    for c in range(width):
        out_ref[:, pl.ds(c * 2 * outputs, 2 * outputs)] = both[c]

    for d in range(1, n_tm):
        s = lax.rem(me + d, n_tm)
        main_copy(s).wait_send()
        part_copy(s).wait_send()

    @pl.when(has_below)
    def _():
        for s in range(n_tm):
            down_copy(s).wait_send()
        row_copy(0, rows, 0, below).wait_send()

    @pl.when(has_above)
    def _():
        for s in range(n_tm):
            up_copy(s).wait_send()
        row_copy(1, 1, rows + 1, above).wait_send()


def local(n_tm, n_rows, latent, gain_first, conv_first, bias_first, conv_upper, bias_upper):
    frames, rows, width, chans = latent.shape
    outputs = conv_upper.shape[2]
    taps, piece, _ = conv_first.shape
    cells = frames * rows * width
    all_frames = n_tm * frames
    depth = rows + 4
    vmem = pl.BlockSpec(memory_space=pltpu.VMEM)
    hbm = pl.BlockSpec(memory_space=pl.ANY)
    dma = pltpu.SemaphoreType.DMA
    flops = 2 * taps * piece * chans * all_frames * rows * width + 18 * 4 * cells * chans * outputs
    both_biases = jnp.concatenate([bias_upper, bias_upper])
    small = jnp.concatenate(
        [
            jnp.broadcast_to(row.reshape(1, 2 * outputs), (8, 2 * outputs))
            for row in (gain_first, bias_first, both_biases)
        ]
    )
    decoded = pl.pallas_call(
        functools.partial(kernel, n_tm, n_rows),
        out_shape=jax.ShapeDtypeStruct((frames * 2 * rows, 2 * width * outputs), BF16),
        in_specs=[vmem, vmem, hbm, hbm],
        out_specs=vmem,
        scratch_shapes=[
            pltpu.VMEM(conv_first.shape, BF16),
            pltpu.VMEM((taps * LANES, chans), BF16),
            pltpu.VMEM((9, outputs, chans), BF16),
            pltpu.VMEM((n_tm, frames, rows, width, LANES), BF16),
            pltpu.VMEM((all_frames, rows + 2, width, LANES), BF16),
            pltpu.VMEM((3, all_frames + 2, rows + 2, width, LANES), BF16),
            pltpu.VMEM((n_tm, cells, chans), BF16),
            pltpu.VMEM((n_tm, cells, chans), BF16),
            pltpu.VMEM((2, cells, chans), F32),
            pltpu.VMEM((frames, depth, width, chans), BF16),
            pltpu.VMEM((6 * cells, frames * depth * width), BF16),
            dma((2,)),
            dma((3 * n_tm,)),
            dma((3 * n_tm,)),
            dma((n_tm,)),
            dma((n_tm,)),
            dma((2,)),
            dma((2,)),
        ],
        compiler_params=pltpu.CompilerParams(
            collective_id=0, has_side_effects=True, vmem_limit_bytes=60 * 1024 * 1024
        ),
        cost_estimate=pl.CostEstimate(
            flops=flops, bytes_accessed=4 * 1024 * 1024, transcendentals=cells * chans
        ),
    )(
        latent,
        small,
        conv_first,
        jnp.swapaxes(conv_upper, 1, 2),
    )
    return decoded.reshape(frames, 2 * rows, 2 * width * outputs)


def solution(mesh):
    in_specs = (P("tm", "rows", None, None), P(), P(None, "tm", None), P(), P(), P())
    out_specs = P("tm", "rows", None)
    body = functools.partial(local, mesh.shape["tm"], mesh.shape["rows"])
    return jax.shard_map(body, mesh=mesh, in_specs=in_specs, out_specs=out_specs, check_vma=False)
```

```python
import functools

import jax
import jax.numpy as jnp
from jax import lax
from jax.experimental import pallas as pl
from jax.experimental.pallas import tpu as pltpu
from jax.sharding import PartitionSpec as P

MESH = pl.DeviceIdType.MESH
F32 = jnp.float32
BF16 = jnp.bfloat16
LANES = 128


def kernel(
    n_tm,
    n_rows,
    latent_ref,
    gain_ref,
    bias1_ref,
    bias2_ref,
    w1_hbm,
    wu_hbm,
    out_ref,
    w1_ref,
    wpad,
    wu_ref,
    send,
    recv,
    shifted,
    part_send,
    part_recv,
    own,
    block,
    pick,
    load_sem,
    act_send_sem,
    act_recv_sem,
    part_send_sem,
    part_recv_sem,
    row_send_sem,
    row_recv_sem,
):
    frames, rows, width, chans = latent_ref.shape
    cells = frames * rows * width
    taps, piece, _ = w1_ref.shape
    outputs = wu_ref.shape[1]
    me = lax.axis_index("tm")
    band = lax.axis_index("rows")
    above = lax.rem(band + n_rows - 1, n_rows)
    below = lax.rem(band + 1, n_rows)
    has_above = band > 0
    has_below = band < n_rows - 1

    load_w1 = pltpu.make_async_copy(w1_hbm, w1_ref, load_sem.at[0])
    load_w1.start()
    load_wu = pltpu.make_async_copy(wu_hbm, wu_ref, load_sem.at[1])
    load_wu.start()

    barrier = pltpu.get_barrier_semaphore()
    for d in range(1, n_tm):
        pl.semaphore_signal(
            barrier, inc=1, device_id=(lax.rem(me + d, n_tm), band), device_id_type=MESH
        )

    @pl.when(has_above)
    def _():
        for s in range(n_tm):
            pl.semaphore_signal(barrier, inc=1, device_id=(s, above), device_id_type=MESH)

    @pl.when(has_below)
    def _():
        for s in range(n_tm):
            pl.semaphore_signal(barrier, inc=1, device_id=(s, below), device_id_type=MESH)

    values = latent_ref[...].astype(F32).reshape(cells, chans)
    mean_square = jnp.mean(values * values, axis=-1, keepdims=True)
    scaled = values * lax.rsqrt(mean_square + 1e-06) * gain_ref[...].reshape(1, chans)
    act = scaled / (1.0 + jnp.exp(-scaled))
    blank = jnp.zeros((cells, LANES - piece), F32)
    for s in range(n_tm):
        cut = jnp.concatenate([act[:, s * piece : (s + 1) * piece], blank], axis=1)
        send[s] = cut.astype(BF16).reshape(frames, rows, width, LANES)

    neighbours = jnp.where(has_above, n_tm, 0) + jnp.where(has_below, n_tm, 0)
    pl.semaphore_wait(barrier, n_tm - 1 + neighbours)

    mine = pl.ds(me * frames, frames)

    def act_copy(s, kind, row, where, to):
        return pltpu.make_async_remote_copy(
            src_ref=send.at[s, :, row],
            dst_ref=recv.at[mine, where],
            send_sem=act_send_sem.at[3 * s + kind],
            recv_sem=act_recv_sem.at[3 * me + kind],
            device_id=(s, to),
            device_id_type=MESH,
        )

    def main_copy(s):
        return act_copy(s, 0, pl.ds(0, rows), pl.ds(1, rows), band)

    def down_copy(s):
        return act_copy(s, 1, pl.ds(rows - 1, 1), pl.ds(0, 1), below)

    def up_copy(s):
        return act_copy(s, 2, pl.ds(0, 1), pl.ds(rows + 1, 1), above)

    for d in range(1, n_tm):
        main_copy(lax.rem(me + d, n_tm)).start()

    @pl.when(has_below)
    def _():
        for s in range(n_tm):
            down_copy(s).start()

    @pl.when(has_above)
    def _():
        for s in range(n_tm):
            up_copy(s).start()

    recv[mine, pl.ds(1, rows)] = send[me]
    all_frames = n_tm * frames
    edge = jnp.zeros((all_frames, 1, width, LANES), BF16)
    block_edge = jnp.zeros((frames, 1, width, chans), BF16)

    @pl.when(band == 0)
    def _():
        recv[:, pl.ds(0, 1)] = edge
        block[:, pl.ds(0, 1)] = block_edge

    @pl.when(band == n_rows - 1)
    def _():
        recv[:, pl.ds(rows + 1, 1)] = edge
        block[:, pl.ds(rows + 1, 1)] = block_edge

    shifted[:, pl.ds(0, 2)] = jnp.zeros((3, 2, rows + 2, width, LANES), BF16)

    big = 2 * rows
    depth = block.shape[1]
    block[:, pl.ds(rows + 2, depth - rows - 2)] = jnp.zeros(
        (frames, depth - rows - 2, width, chans), BF16
    )
    at = lax.broadcasted_iota(jnp.int32, (pick.shape[0], 1), 0)
    to = lax.broadcasted_iota(jnp.int32, pick.shape, 1)
    row_tap = at // (frames * width * big)
    col = (at // (frames * big)) % width
    frame = (at // big) % frames
    line = at % big
    source = frame * (depth * width) + ((line + row_tap + 1) // 2) * width + col
    pick[...] = jnp.where(to == source, 1.0, 0.0).astype(BF16)

    load_w1.wait()
    spare = jnp.zeros((LANES - piece, chans), BF16)
    for tap in range(taps):
        wpad[pl.ds(tap * LANES, LANES)] = jnp.concatenate([w1_ref[tap], spare], axis=0)

    def act_arrival(s, kind, row, where):
        return pltpu.make_async_remote_copy(
            src_ref=send.at[s, :, row],
            dst_ref=recv.at[pl.ds(s * frames, frames), where],
            send_sem=act_send_sem.at[3 * s + kind],
            recv_sem=act_recv_sem.at[3 * s + kind],
            device_id=(lax.rem(me + 1, n_tm), band),
            device_id_type=MESH,
        )

    for d in range(1, n_tm):
        s = lax.rem(me + d, n_tm)
        act_arrival(s, 0, pl.ds(0, rows), pl.ds(1, rows)).wait_recv()

    @pl.when(has_above)
    def _():
        for s in range(n_tm):
            act_arrival(s, 1, pl.ds(0, 1), pl.ds(0, 1)).wait_recv()

    @pl.when(has_below)
    def _():
        for s in range(n_tm):
            act_arrival(s, 2, pl.ds(0, 1), pl.ds(rows + 1, 1)).wait_recv()

    tall = all_frames * (rows + 2) * width
    flat = recv[...].astype(F32).reshape(tall, LANES)
    column = lax.broadcasted_iota(jnp.int32, (tall, LANES), 0) % width
    left = jnp.where(column == 0, 0.0, pltpu.roll(flat, 1, 0))
    right = jnp.where(column == width - 1, 0.0, pltpu.roll(flat, tall - 1, 0))
    shape = (all_frames, rows + 2, width, LANES)
    shifted[0, pl.ds(2, all_frames)] = left.astype(BF16).reshape(shape)
    shifted[1, pl.ds(2, all_frames)] = recv[...]
    shifted[2, pl.ds(2, all_frames)] = right.astype(BF16).reshape(shape)

    pairs = n_tm // 2

    def part_copy(s):
        return pltpu.make_async_remote_copy(
            src_ref=part_send.at[s],
            dst_ref=part_recv.at[me],
            send_sem=part_send_sem.at[s],
            recv_sem=part_recv_sem.at[me],
            device_id=(s, band),
            device_id_type=MESH,
        )

    for k in range(1, pairs + 1):
        pair = lax.rem(lax.div(me, 2) + k, pairs)
        total = jnp.zeros((2 * cells, chans), F32)
        for dt in range(3):
            windows = []
            for dy in range(3):
                for dx in range(3):
                    start = pair * (2 * frames) + dt
                    view = shifted[dx, pl.ds(start, 2 * frames), pl.ds(dy, rows)]
                    windows.append(view.reshape(2 * cells, LANES))
            total = total + jnp.dot(
                jnp.concatenate(windows, axis=1),
                wpad[pl.ds(dt * 9 * LANES, 9 * LANES)],
                preferred_element_type=F32,
            )
        if k < pairs:
            for c in range(2):
                part_send[2 * pair + c] = total[c * cells : (c + 1) * cells].astype(BF16)
                part_copy(2 * pair + c).start()
        else:
            own[...] = total.reshape(2, cells, chans)
            mate = 2 * lax.div(me, 2) + (1 - lax.rem(me, 2))
            part_send[mate] = own[1 - lax.rem(me, 2)].astype(BF16)
            part_copy(mate).start()

    summed = own[lax.rem(me, 2)] + bias1_ref[...].reshape(1, chans)
    summed = summed + latent_ref[...].astype(F32).reshape(cells, chans)
    for d in range(1, n_tm):
        s = lax.rem(me + n_tm - d, n_tm)
        pltpu.make_async_remote_copy(
            src_ref=part_send.at[s],
            dst_ref=part_recv.at[s],
            send_sem=part_send_sem.at[s],
            recv_sem=part_recv_sem.at[s],
            device_id=(s, band),
            device_id_type=MESH,
        ).wait_recv()
        summed = summed + part_recv[s].astype(F32)
    block[:, pl.ds(1, rows)] = summed.astype(BF16).reshape(frames, rows, width, chans)

    def row_copy(kind, row, where, to):
        return pltpu.make_async_remote_copy(
            src_ref=block.at[:, pl.ds(row, 1)],
            dst_ref=block.at[:, pl.ds(where, 1)],
            send_sem=row_send_sem.at[kind],
            recv_sem=row_recv_sem.at[kind],
            device_id=(me, to),
            device_id_type=MESH,
        )

    @pl.when(has_below)
    def _():
        row_copy(0, rows, 0, below).start()

    @pl.when(has_above)
    def _():
        row_copy(1, 1, rows + 1, above).start()

    load_wu.wait()

    @pl.when(has_above)
    def _():
        row_copy(0, rows, 0, above).wait_recv()

    @pl.when(has_below)
    def _():
        row_copy(1, 1, rows + 1, below).wait_recv()

    spread = jnp.dot(
        pick[...],
        block[...].reshape(frames * depth * width, chans),
        preferred_element_type=F32,
    ).astype(BF16)
    high = frames * width * big
    lines = jnp.concatenate([spread[k * high : (k + 1) * high] for k in range(3)], axis=1)
    cols = []
    for dx in range(3):
        weights = jnp.concatenate([wu_ref[dx], wu_ref[3 + dx], wu_ref[6 + dx]], axis=1)
        product = lax.dot_general(
            lines, weights, (((1,), (1,)), ((), ())), preferred_element_type=F32
        )
        cols.append(product.reshape(width, frames * big, outputs))
    nothing = jnp.zeros((1, frames * big, outputs), F32)
    before = jnp.concatenate([nothing, cols[0][: width - 1]], axis=0)
    after = jnp.concatenate([cols[2][1:], nothing], axis=0)
    bias2 = bias2_ref[...].reshape(1, 1, outputs)
    even = before + cols[1] + cols[2] + bias2
    odd = cols[0] + cols[1] + after + bias2
    both = jnp.concatenate([even, odd], axis=-1).astype(BF16)
    for c in range(width):
        out_ref[:, pl.ds(c * 2 * outputs, 2 * outputs)] = both[c]

    for d in range(1, n_tm):
        s = lax.rem(me + d, n_tm)
        main_copy(s).wait_send()
        part_copy(s).wait_send()

    @pl.when(has_below)
    def _():
        for s in range(n_tm):
            down_copy(s).wait_send()
        row_copy(0, rows, 0, below).wait_send()

    @pl.when(has_above)
    def _():
        for s in range(n_tm):
            up_copy(s).wait_send()
        row_copy(1, 1, rows + 1, above).wait_send()


def local(n_tm, n_rows, latent, gain_first, conv_first, bias_first, conv_upper, bias_upper):
    frames, rows, width, chans = latent.shape
    outputs = conv_upper.shape[2]
    taps, piece, _ = conv_first.shape
    cells = frames * rows * width
    all_frames = n_tm * frames
    depth = rows + 4
    vmem = pl.BlockSpec(memory_space=pltpu.VMEM)
    hbm = pl.BlockSpec(memory_space=pltpu.HBM)
    dma = pltpu.SemaphoreType.DMA
    flops = 2 * taps * piece * chans * all_frames * rows * width + 18 * 4 * cells * chans * outputs
    decoded = pl.pallas_call(
        functools.partial(kernel, n_tm, n_rows),
        out_shape=jax.ShapeDtypeStruct((frames * 2 * rows, 2 * width * outputs), BF16),
        in_specs=[vmem, vmem, vmem, vmem, hbm, hbm],
        out_specs=vmem,
        scratch_shapes=[
            pltpu.VMEM(conv_first.shape, BF16),
            pltpu.VMEM((taps * LANES, chans), BF16),
            pltpu.VMEM((9, outputs, chans), BF16),
            pltpu.VMEM((n_tm, frames, rows, width, LANES), BF16),
            pltpu.VMEM((all_frames, rows + 2, width, LANES), BF16),
            pltpu.VMEM((3, all_frames + 2, rows + 2, width, LANES), BF16),
            pltpu.VMEM((n_tm, cells, chans), BF16),
            pltpu.VMEM((n_tm, cells, chans), BF16),
            pltpu.VMEM((2, cells, chans), F32),
            pltpu.VMEM((frames, depth, width, chans), BF16),
            pltpu.VMEM((6 * cells, frames * depth * width), BF16),
            dma((2,)),
            dma((3 * n_tm,)),
            dma((3 * n_tm,)),
            dma((n_tm,)),
            dma((n_tm,)),
            dma((2,)),
            dma((2,)),
        ],
        compiler_params=pltpu.CompilerParams(
            collective_id=0, has_side_effects=True, vmem_limit_bytes=60 * 1024 * 1024
        ),
        cost_estimate=pl.CostEstimate(
            flops=flops, bytes_accessed=4 * 1024 * 1024, transcendentals=cells * chans
        ),
    )(
        latent,
        gain_first,
        bias_first,
        bias_upper,
        conv_first,
        jnp.swapaxes(conv_upper, 1, 2),
    )
    return decoded.reshape(frames, 2 * rows, 2 * width * outputs)


def solution(mesh):
    in_specs = (P("tm", "rows", None, None), P(), P(None, "tm", None), P(), P(), P())
    out_specs = P("tm", "rows", None)
    body = functools.partial(local, mesh.shape["tm"], mesh.shape["rows"])
    return jax.shard_map(body, mesh=mesh, in_specs=in_specs, out_specs=out_specs, check_vma=False)
```

```python
import functools

import jax
import jax.numpy as jnp
from jax import lax
from jax.experimental import pallas as pl
from jax.experimental.pallas import tpu as pltpu
from jax.sharding import PartitionSpec as P

MESH = pl.DeviceIdType.MESH
F32 = jnp.float32
BF16 = jnp.bfloat16
LANES = 128


def kernel(
    n_tm,
    n_rows,
    latent_ref,
    gain_ref,
    bias1_ref,
    bias2_ref,
    w1_hbm,
    wu_hbm,
    out_ref,
    w1_ref,
    wpad,
    wu_ref,
    send,
    recv,
    shifted,
    part_send,
    part_recv,
    own,
    block,
    pick,
    load_sem,
    act_send_sem,
    act_recv_sem,
    part_send_sem,
    part_recv_sem,
    row_send_sem,
    row_recv_sem,
):
    frames, rows, width, chans = latent_ref.shape
    cells = frames * rows * width
    taps, piece, _ = w1_ref.shape
    outputs = wu_ref.shape[1]
    me = lax.axis_index("tm")
    band = lax.axis_index("rows")
    above = lax.rem(band + n_rows - 1, n_rows)
    below = lax.rem(band + 1, n_rows)
    has_above = band > 0
    has_below = band < n_rows - 1

    load_w1 = pltpu.make_async_copy(w1_hbm, w1_ref, load_sem.at[0])
    load_w1.start()
    load_wu = pltpu.make_async_copy(wu_hbm, wu_ref, load_sem.at[1])
    load_wu.start()

    barrier = pltpu.get_barrier_semaphore()
    for d in range(1, n_tm):
        pl.semaphore_signal(
            barrier, inc=1, device_id=(lax.rem(me + d, n_tm), band), device_id_type=MESH
        )

    @pl.when(has_above)
    def _():
        for s in range(n_tm):
            pl.semaphore_signal(barrier, inc=1, device_id=(s, above), device_id_type=MESH)

    @pl.when(has_below)
    def _():
        for s in range(n_tm):
            pl.semaphore_signal(barrier, inc=1, device_id=(s, below), device_id_type=MESH)

    values = latent_ref[...].astype(F32).reshape(cells, chans)
    mean_square = jnp.mean(values * values, axis=-1, keepdims=True)
    scaled = values * lax.rsqrt(mean_square + 1e-06) * gain_ref[...].reshape(1, chans)
    act = scaled / (1.0 + jnp.exp(-scaled))
    blank = jnp.zeros((cells, LANES - piece), F32)
    for s in range(n_tm):
        cut = jnp.concatenate([act[:, s * piece : (s + 1) * piece], blank], axis=1)
        send[s] = cut.astype(BF16).reshape(frames, rows, width, LANES)

    neighbours = jnp.where(has_above, n_tm, 0) + jnp.where(has_below, n_tm, 0)
    pl.semaphore_wait(barrier, n_tm - 1 + neighbours)

    mine = pl.ds(me * frames, frames)

    def act_copy(s, kind, row, where, to):
        return pltpu.make_async_remote_copy(
            src_ref=send.at[s, :, row],
            dst_ref=recv.at[mine, where],
            send_sem=act_send_sem.at[3 * s + kind],
            recv_sem=act_recv_sem.at[3 * me + kind],
            device_id=(s, to),
            device_id_type=MESH,
        )

    def main_copy(s):
        return act_copy(s, 0, pl.ds(0, rows), pl.ds(1, rows), band)

    def down_copy(s):
        return act_copy(s, 1, pl.ds(rows - 1, 1), pl.ds(0, 1), below)

    def up_copy(s):
        return act_copy(s, 2, pl.ds(0, 1), pl.ds(rows + 1, 1), above)

    for d in range(1, n_tm):
        main_copy(lax.rem(me + d, n_tm)).start()

    @pl.when(has_below)
    def _():
        for s in range(n_tm):
            down_copy(s).start()

    @pl.when(has_above)
    def _():
        for s in range(n_tm):
            up_copy(s).start()

    recv[mine, pl.ds(1, rows)] = send[me]
    all_frames = n_tm * frames
    edge = jnp.zeros((all_frames, 1, width, LANES), BF16)
    block_edge = jnp.zeros((frames, 1, width, chans), BF16)

    @pl.when(band == 0)
    def _():
        recv[:, pl.ds(0, 1)] = edge
        block[:, pl.ds(0, 1)] = block_edge

    @pl.when(band == n_rows - 1)
    def _():
        recv[:, pl.ds(rows + 1, 1)] = edge
        block[:, pl.ds(rows + 1, 1)] = block_edge

    shifted[:, pl.ds(0, 2)] = jnp.zeros((3, 2, rows + 2, width, LANES), BF16)

    big = 2 * rows
    depth = block.shape[1]
    block[:, pl.ds(rows + 2, depth - rows - 2)] = jnp.zeros(
        (frames, depth - rows - 2, width, chans), BF16
    )
    at = lax.broadcasted_iota(jnp.int32, (pick.shape[0], 1), 0)
    to = lax.broadcasted_iota(jnp.int32, pick.shape, 1)
    row_tap = at // (frames * width * big)
    col = (at // (frames * big)) % width
    frame = (at // big) % frames
    line = at % big
    source = frame * (depth * width) + ((line + row_tap + 1) // 2) * width + col
    pick[...] = jnp.where(to == source, 1.0, 0.0).astype(BF16)

    load_w1.wait()
    spare = jnp.zeros((LANES - piece, chans), BF16)
    for tap in range(taps):
        wpad[pl.ds(tap * LANES, LANES)] = jnp.concatenate([w1_ref[tap], spare], axis=0)

    def act_arrival(s, kind, row, where):
        return pltpu.make_async_remote_copy(
            src_ref=send.at[s, :, row],
            dst_ref=recv.at[pl.ds(s * frames, frames), where],
            send_sem=act_send_sem.at[3 * s + kind],
            recv_sem=act_recv_sem.at[3 * s + kind],
            device_id=(lax.rem(me + 1, n_tm), band),
            device_id_type=MESH,
        )

    for d in range(1, n_tm):
        s = lax.rem(me + d, n_tm)
        act_arrival(s, 0, pl.ds(0, rows), pl.ds(1, rows)).wait_recv()

    @pl.when(has_above)
    def _():
        for s in range(n_tm):
            act_arrival(s, 1, pl.ds(0, 1), pl.ds(0, 1)).wait_recv()

    @pl.when(has_below)
    def _():
        for s in range(n_tm):
            act_arrival(s, 2, pl.ds(0, 1), pl.ds(rows + 1, 1)).wait_recv()

    tall = all_frames * (rows + 2) * width
    flat = recv[...].astype(F32).reshape(tall, LANES)
    column = lax.broadcasted_iota(jnp.int32, (tall, LANES), 0) % width
    left = jnp.where(column == 0, 0.0, pltpu.roll(flat, 1, 0))
    right = jnp.where(column == width - 1, 0.0, pltpu.roll(flat, tall - 1, 0))
    shape = (all_frames, rows + 2, width, LANES)
    shifted[0, pl.ds(2, all_frames)] = left.astype(BF16).reshape(shape)
    shifted[1, pl.ds(2, all_frames)] = recv[...]
    shifted[2, pl.ds(2, all_frames)] = right.astype(BF16).reshape(shape)

    pairs = n_tm // 2

    order = [0, rows - 1] + list(range(1, rows - 1))
    spans = (pl.ds(0, 2), pl.ds(2, rows - 2))

    def part_copy(s, kind):
        return pltpu.make_async_remote_copy(
            src_ref=part_send.at[s, :, spans[kind]],
            dst_ref=part_recv.at[me, :, spans[kind]],
            send_sem=part_send_sem.at[2 * s + kind],
            recv_sem=part_recv_sem.at[2 * me + kind],
            device_id=(s, band),
            device_id_type=MESH,
        )

    def part_arrival(s, kind):
        return pltpu.make_async_remote_copy(
            src_ref=part_send.at[s, :, spans[kind]],
            dst_ref=part_recv.at[s, :, spans[kind]],
            send_sem=part_send_sem.at[2 * s + kind],
            recv_sem=part_recv_sem.at[2 * s + kind],
            device_id=(s, band),
            device_id_type=MESH,
        )

    def stage(s, sums):
        for slot, row in enumerate(order):
            part_send[s, :, slot] = sums[:, row].astype(BF16)

    for k in range(1, pairs + 1):
        pair = lax.rem(lax.div(me, 2) + k, pairs)
        total = jnp.zeros((2 * cells, chans), F32)
        for dt in range(3):
            windows = []
            for dy in range(3):
                for dx in range(3):
                    start = pair * (2 * frames) + dt
                    view = shifted[dx, pl.ds(start, 2 * frames), pl.ds(dy, rows)]
                    windows.append(view.reshape(2 * cells, LANES))
            total = total + jnp.dot(
                jnp.concatenate(windows, axis=1),
                wpad[pl.ds(dt * 9 * LANES, 9 * LANES)],
                preferred_element_type=F32,
            )
        sums = total.reshape(2, frames, rows, width, chans)
        if k < pairs:
            for c in range(2):
                stage(2 * pair + c, sums[c])
            for kind in range(2):
                for c in range(2):
                    part_copy(2 * pair + c, kind).start()
        else:
            own[...] = sums
            mate = 2 * lax.div(me, 2) + (1 - lax.rem(me, 2))
            stage(mate, own[1 - lax.rem(me, 2)])
            for kind in range(2):
                part_copy(mate, kind).start()

    bias1 = bias1_ref[...].reshape(1, 1, chans)

    def finish(kind):
        for d in range(1, n_tm):
            part_arrival(lax.rem(me + n_tm - d, n_tm), kind).wait_recv()
        for slot, row in enumerate(order):
            if (slot >= 2) != (kind == 1):
                continue
            summed = own[lax.rem(me, 2), :, row] + bias1 + latent_ref[:, row].astype(F32)
            for d in range(1, n_tm):
                summed = summed + part_recv[lax.rem(me + n_tm - d, n_tm), :, slot].astype(F32)
            block[:, row + 1] = summed.astype(BF16)

    finish(0)

    def row_copy(kind, row, where, to):
        return pltpu.make_async_remote_copy(
            src_ref=block.at[:, pl.ds(row, 1)],
            dst_ref=block.at[:, pl.ds(where, 1)],
            send_sem=row_send_sem.at[kind],
            recv_sem=row_recv_sem.at[kind],
            device_id=(me, to),
            device_id_type=MESH,
        )

    @pl.when(has_below)
    def _():
        row_copy(0, rows, 0, below).start()

    @pl.when(has_above)
    def _():
        row_copy(1, 1, rows + 1, above).start()

    finish(1)
    load_wu.wait()

    @pl.when(has_above)
    def _():
        row_copy(0, rows, 0, above).wait_recv()

    @pl.when(has_below)
    def _():
        row_copy(1, 1, rows + 1, below).wait_recv()

    spread = jnp.dot(
        pick[...],
        block[...].reshape(frames * depth * width, chans),
        preferred_element_type=F32,
    ).astype(BF16)
    high = frames * width * big
    lines = jnp.concatenate([spread[k * high : (k + 1) * high] for k in range(3)], axis=1)
    cols = []
    for dx in range(3):
        weights = jnp.concatenate([wu_ref[dx], wu_ref[3 + dx], wu_ref[6 + dx]], axis=1)
        product = lax.dot_general(
            lines, weights, (((1,), (1,)), ((), ())), preferred_element_type=F32
        )
        cols.append(product.reshape(width, frames * big, outputs))
    nothing = jnp.zeros((1, frames * big, outputs), F32)
    before = jnp.concatenate([nothing, cols[0][: width - 1]], axis=0)
    after = jnp.concatenate([cols[2][1:], nothing], axis=0)
    bias2 = bias2_ref[...].reshape(1, 1, outputs)
    even = before + cols[1] + cols[2] + bias2
    odd = cols[0] + cols[1] + after + bias2
    both = jnp.concatenate([even, odd], axis=-1).astype(BF16)
    for c in range(width):
        out_ref[:, pl.ds(c * 2 * outputs, 2 * outputs)] = both[c]

    for d in range(1, n_tm):
        s = lax.rem(me + d, n_tm)
        main_copy(s).wait_send()
        for kind in range(2):
            part_copy(s, kind).wait_send()

    @pl.when(has_below)
    def _():
        for s in range(n_tm):
            down_copy(s).wait_send()
        row_copy(0, rows, 0, below).wait_send()

    @pl.when(has_above)
    def _():
        for s in range(n_tm):
            up_copy(s).wait_send()
        row_copy(1, 1, rows + 1, above).wait_send()


def local(n_tm, n_rows, latent, gain_first, conv_first, bias_first, conv_upper, bias_upper):
    frames, rows, width, chans = latent.shape
    outputs = conv_upper.shape[2]
    taps, piece, _ = conv_first.shape
    cells = frames * rows * width
    all_frames = n_tm * frames
    depth = rows + 4
    vmem = pl.BlockSpec(memory_space=pltpu.VMEM)
    hbm = pl.BlockSpec(memory_space=pltpu.HBM)
    dma = pltpu.SemaphoreType.DMA
    flops = 2 * taps * piece * chans * all_frames * rows * width + 18 * 4 * cells * chans * outputs
    decoded = pl.pallas_call(
        functools.partial(kernel, n_tm, n_rows),
        out_shape=jax.ShapeDtypeStruct((frames * 2 * rows, 2 * width * outputs), BF16),
        in_specs=[vmem, vmem, vmem, vmem, hbm, hbm],
        out_specs=vmem,
        scratch_shapes=[
            pltpu.VMEM(conv_first.shape, BF16),
            pltpu.VMEM((taps * LANES, chans), BF16),
            pltpu.VMEM((9, outputs, chans), BF16),
            pltpu.VMEM((n_tm, frames, rows, width, LANES), BF16),
            pltpu.VMEM((all_frames, rows + 2, width, LANES), BF16),
            pltpu.VMEM((3, all_frames + 2, rows + 2, width, LANES), BF16),
            pltpu.VMEM((n_tm, frames, rows, width, chans), BF16),
            pltpu.VMEM((n_tm, frames, rows, width, chans), BF16),
            pltpu.VMEM((2, frames, rows, width, chans), F32),
            pltpu.VMEM((frames, depth, width, chans), BF16),
            pltpu.VMEM((6 * cells, frames * depth * width), BF16),
            dma((2,)),
            dma((3 * n_tm,)),
            dma((3 * n_tm,)),
            dma((2 * n_tm,)),
            dma((2 * n_tm,)),
            dma((2,)),
            dma((2,)),
        ],
        compiler_params=pltpu.CompilerParams(
            collective_id=0, has_side_effects=True, vmem_limit_bytes=60 * 1024 * 1024
        ),
        cost_estimate=pl.CostEstimate(
            flops=flops, bytes_accessed=4 * 1024 * 1024, transcendentals=cells * chans
        ),
    )(
        latent,
        gain_first,
        bias_first,
        bias_upper,
        conv_first,
        jnp.swapaxes(conv_upper, 1, 2),
    )
    return decoded.reshape(frames, 2 * rows, 2 * width * outputs)


def solution(mesh):
    in_specs = (P("tm", "rows", None, None), P(), P(None, "tm", None), P(), P(), P())
    out_specs = P("tm", "rows", None)
    body = functools.partial(local, mesh.shape["tm"], mesh.shape["rows"])
    return jax.shard_map(body, mesh=mesh, in_specs=in_specs, out_specs=out_specs, check_vma=False)
```

```python
import functools

import jax
import jax.numpy as jnp
from jax import lax
from jax.experimental import pallas as pl
from jax.experimental.pallas import tpu as pltpu
from jax.sharding import PartitionSpec as P

MESH = pl.DeviceIdType.MESH
F32 = jnp.float32
BF16 = jnp.bfloat16
LANES = 128


def kernel(
    n_tm,
    n_rows,
    latent_ref,
    gain_ref,
    bias1_ref,
    bias2_ref,
    w1_hbm,
    wu_hbm,
    out_ref,
    w1_ref,
    wpad,
    wu_ref,
    send,
    recv,
    shifted,
    part_send,
    part_recv,
    own,
    block,
    pick,
    load_sem,
    act_send_sem,
    act_recv_sem,
    part_send_sem,
    part_recv_sem,
    row_send_sem,
    row_recv_sem,
):
    frames, rows, width, chans = latent_ref.shape
    cells = frames * rows * width
    taps, piece, _ = w1_ref.shape
    outputs = wu_ref.shape[1]
    me = lax.axis_index("tm")
    band = lax.axis_index("rows")
    above = lax.rem(band + n_rows - 1, n_rows)
    below = lax.rem(band + 1, n_rows)
    has_above = band > 0
    has_below = band < n_rows - 1

    load_w1 = pltpu.make_async_copy(w1_hbm, w1_ref, load_sem.at[0])
    load_w1.start()
    load_wu = pltpu.make_async_copy(wu_hbm, wu_ref, load_sem.at[1])
    load_wu.start()

    barrier = pltpu.get_barrier_semaphore()
    for d in range(1, n_tm):
        pl.semaphore_signal(
            barrier, inc=1, device_id=(lax.rem(me + d, n_tm), band), device_id_type=MESH
        )

    @pl.when(has_above)
    def _():
        for s in range(n_tm):
            pl.semaphore_signal(barrier, inc=1, device_id=(s, above), device_id_type=MESH)

    @pl.when(has_below)
    def _():
        for s in range(n_tm):
            pl.semaphore_signal(barrier, inc=1, device_id=(s, below), device_id_type=MESH)

    values = latent_ref[...].astype(F32).reshape(cells, chans)
    mean_square = jnp.mean(values * values, axis=-1, keepdims=True)
    scaled = values * lax.rsqrt(mean_square + 1e-06) * gain_ref[...].reshape(1, chans)
    act = scaled / (1.0 + jnp.exp(-scaled))
    blank = jnp.zeros((cells, LANES - piece), F32)
    for s in range(n_tm):
        cut = jnp.concatenate([act[:, s * piece : (s + 1) * piece], blank], axis=1)
        send[s] = cut.astype(BF16).reshape(frames, rows, width, LANES)

    neighbours = jnp.where(has_above, n_tm, 0) + jnp.where(has_below, n_tm, 0)
    pl.semaphore_wait(barrier, n_tm - 1 + neighbours)

    mine = pl.ds(me * frames, frames)

    def act_copy(s, kind, row, where, to):
        return pltpu.make_async_remote_copy(
            src_ref=send.at[s, :, row],
            dst_ref=recv.at[mine, where],
            send_sem=act_send_sem.at[3 * s + kind],
            recv_sem=act_recv_sem.at[3 * me + kind],
            device_id=(s, to),
            device_id_type=MESH,
        )

    def main_copy(s):
        return act_copy(s, 0, pl.ds(0, rows), pl.ds(1, rows), band)

    def down_copy(s):
        return act_copy(s, 1, pl.ds(rows - 1, 1), pl.ds(0, 1), below)

    def up_copy(s):
        return act_copy(s, 2, pl.ds(0, 1), pl.ds(rows + 1, 1), above)

    for d in range(1, n_tm):
        main_copy(lax.rem(me + d, n_tm)).start()

    @pl.when(has_below)
    def _():
        for s in range(n_tm):
            down_copy(s).start()

    @pl.when(has_above)
    def _():
        for s in range(n_tm):
            up_copy(s).start()

    recv[mine, pl.ds(1, rows)] = send[me]
    all_frames = n_tm * frames
    edge = jnp.zeros((all_frames, 1, width, LANES), BF16)
    block_edge = jnp.zeros((frames, 1, width, chans), BF16)

    @pl.when(band == 0)
    def _():
        recv[:, pl.ds(0, 1)] = edge
        block[:, pl.ds(0, 1)] = block_edge

    @pl.when(band == n_rows - 1)
    def _():
        recv[:, pl.ds(rows + 1, 1)] = edge
        block[:, pl.ds(rows + 1, 1)] = block_edge

    shifted[:, pl.ds(0, 2)] = jnp.zeros((3, 2, rows + 2, width, LANES), BF16)

    big = 2 * rows
    depth = block.shape[1]
    block[:, pl.ds(rows + 2, depth - rows - 2)] = jnp.zeros(
        (frames, depth - rows - 2, width, chans), BF16
    )
    at = lax.broadcasted_iota(jnp.int32, (pick.shape[0], 1), 0)
    to = lax.broadcasted_iota(jnp.int32, pick.shape, 1)
    row_tap = at // (frames * width * big)
    col = (at // (frames * big)) % width
    frame = (at // big) % frames
    line = at % big
    source = frame * (depth * width) + ((line + row_tap + 1) // 2) * width + col
    pick[...] = jnp.where(to == source, 1.0, 0.0).astype(BF16)

    load_w1.wait()
    spare = jnp.zeros((LANES - piece, chans), BF16)
    for tap in range(taps):
        wpad[pl.ds(tap * LANES, LANES)] = jnp.concatenate([w1_ref[tap], spare], axis=0)

    def act_arrival(s, kind, row, where):
        return pltpu.make_async_remote_copy(
            src_ref=send.at[s, :, row],
            dst_ref=recv.at[pl.ds(s * frames, frames), where],
            send_sem=act_send_sem.at[3 * s + kind],
            recv_sem=act_recv_sem.at[3 * s + kind],
            device_id=(lax.rem(me + 1, n_tm), band),
            device_id_type=MESH,
        )

    for d in range(1, n_tm):
        s = lax.rem(me + d, n_tm)
        act_arrival(s, 0, pl.ds(0, rows), pl.ds(1, rows)).wait_recv()

    @pl.when(has_above)
    def _():
        for s in range(n_tm):
            act_arrival(s, 1, pl.ds(0, 1), pl.ds(0, 1)).wait_recv()

    @pl.when(has_below)
    def _():
        for s in range(n_tm):
            act_arrival(s, 2, pl.ds(0, 1), pl.ds(rows + 1, 1)).wait_recv()

    tall = all_frames * (rows + 2) * width
    flat = recv[...].astype(F32).reshape(tall, LANES)
    column = lax.broadcasted_iota(jnp.int32, (tall, LANES), 0) % width
    left = jnp.where(column == 0, 0.0, pltpu.roll(flat, 1, 0))
    right = jnp.where(column == width - 1, 0.0, pltpu.roll(flat, tall - 1, 0))
    shape = (all_frames, rows + 2, width, LANES)
    shifted[0, pl.ds(2, all_frames)] = left.astype(BF16).reshape(shape)
    shifted[1, pl.ds(2, all_frames)] = recv[...]
    shifted[2, pl.ds(2, all_frames)] = right.astype(BF16).reshape(shape)

    pairs = n_tm // 2

    order = [0, rows - 1] + list(range(1, rows - 1))
    spans = (pl.ds(0, 2), pl.ds(2, rows - 2))

    def part_copy(s, kind):
        return pltpu.make_async_remote_copy(
            src_ref=part_send.at[s, :, spans[kind]],
            dst_ref=part_recv.at[me, :, spans[kind]],
            send_sem=part_send_sem.at[2 * s + kind],
            recv_sem=part_recv_sem.at[2 * me + kind],
            device_id=(s, band),
            device_id_type=MESH,
        )

    def part_arrival(s, kind):
        return pltpu.make_async_remote_copy(
            src_ref=part_send.at[s, :, spans[kind]],
            dst_ref=part_recv.at[s, :, spans[kind]],
            send_sem=part_send_sem.at[2 * s + kind],
            recv_sem=part_recv_sem.at[2 * s + kind],
            device_id=(s, band),
            device_id_type=MESH,
        )

    def stage(s, sums):
        for slot, row in enumerate(order):
            part_send[s, :, slot] = sums[:, row].astype(BF16)

    for k in range(1, pairs + 1):
        pair = lax.rem(lax.div(me, 2) + k, pairs)
        total = jnp.zeros((2 * cells, chans), F32)
        for dt in range(3):
            windows = []
            for dy in range(3):
                for dx in range(3):
                    start = pair * (2 * frames) + dt
                    view = shifted[dx, pl.ds(start, 2 * frames), pl.ds(dy, rows)]
                    windows.append(view.reshape(2 * cells, LANES))
            total = total + jnp.dot(
                jnp.concatenate(windows, axis=1),
                wpad[pl.ds(dt * 9 * LANES, 9 * LANES)],
                preferred_element_type=F32,
            )
        sums = total.reshape(2, frames, rows, width, chans)
        if k < pairs:
            for c in range(2):
                stage(2 * pair + c, sums[c])
            for kind in range(2):
                for c in range(2):
                    part_copy(2 * pair + c, kind).start()
        else:
            own[...] = sums
            mate = 2 * lax.div(me, 2) + (1 - lax.rem(me, 2))
            stage(mate, own[1 - lax.rem(me, 2)])
            for kind in range(2):
                part_copy(mate, kind).start()

    bias1 = bias1_ref[...].reshape(1, 1, chans)

    def finish(kind):
        for d in range(1, n_tm):
            part_arrival(lax.rem(me + n_tm - d, n_tm), kind).wait_recv()
        for slot, row in enumerate(order):
            if (slot >= 2) != (kind == 1):
                continue
            summed = own[lax.rem(me, 2), :, row] + bias1 + latent_ref[:, row].astype(F32)
            for d in range(1, n_tm):
                summed = summed + part_recv[lax.rem(me + n_tm - d, n_tm), :, slot].astype(F32)
            block[:, row + 1] = summed.astype(BF16)

    finish(0)

    def row_copy(kind, row, where, to):
        return pltpu.make_async_remote_copy(
            src_ref=block.at[:, pl.ds(row, 1)],
            dst_ref=block.at[:, pl.ds(where, 1)],
            send_sem=row_send_sem.at[kind],
            recv_sem=row_recv_sem.at[kind],
            device_id=(me, to),
            device_id_type=MESH,
        )

    @pl.when(has_below)
    def _():
        row_copy(0, rows, 0, below).start()

    @pl.when(has_above)
    def _():
        row_copy(1, 1, rows + 1, above).start()

    finish(1)
    load_wu.wait()

    @pl.when(has_above)
    def _():
        row_copy(0, rows, 0, above).wait_recv()

    @pl.when(has_below)
    def _():
        row_copy(1, 1, rows + 1, below).wait_recv()

    spread = jnp.dot(
        pick[...],
        block[...].reshape(frames * depth * width, chans),
        preferred_element_type=F32,
    ).astype(BF16)
    high = frames * width * big
    lines = jnp.concatenate([spread[k * high : (k + 1) * high] for k in range(3)], axis=1)
    cols = []
    for dx in range(3):
        weights = jnp.concatenate([wu_ref[dx], wu_ref[3 + dx], wu_ref[6 + dx]], axis=1)
        product = lax.dot_general(
            lines, weights, (((1,), (1,)), ((), ())), preferred_element_type=F32
        )
        cols.append(product.reshape(width, frames * big, outputs))
    nothing = jnp.zeros((1, frames * big, outputs), F32)
    before = jnp.concatenate([nothing, cols[0][: width - 1]], axis=0)
    after = jnp.concatenate([cols[2][1:], nothing], axis=0)
    bias2 = bias2_ref[...].reshape(1, 1, outputs)
    even = before + cols[1] + cols[2] + bias2
    odd = cols[0] + cols[1] + after + bias2
    both = jnp.concatenate([even, odd], axis=-1).astype(BF16)
    for c in range(width):
        out_ref[:, pl.ds(c * 2 * outputs, 2 * outputs)] = both[c]

    for d in range(1, n_tm):
        s = lax.rem(me + d, n_tm)
        main_copy(s).wait_send()
        for kind in range(2):
            part_copy(s, kind).wait_send()

    @pl.when(has_below)
    def _():
        for s in range(n_tm):
            down_copy(s).wait_send()
        row_copy(0, rows, 0, below).wait_send()

    @pl.when(has_above)
    def _():
        for s in range(n_tm):
            up_copy(s).wait_send()
        row_copy(1, 1, rows + 1, above).wait_send()


def local(n_tm, n_rows, latent, gain_first, conv_first, bias_first, conv_upper, bias_upper):
    frames, rows, width, chans = latent.shape
    outputs = conv_upper.shape[2]
    taps, piece, _ = conv_first.shape
    cells = frames * rows * width
    all_frames = n_tm * frames
    depth = rows + 4
    vmem = pl.BlockSpec(memory_space=pltpu.VMEM)
    hbm = pl.BlockSpec(memory_space=pltpu.HBM)
    dma = pltpu.SemaphoreType.DMA
    flops = 2 * taps * piece * chans * all_frames * rows * width + 18 * 4 * cells * chans * outputs
    decoded = pl.pallas_call(
        functools.partial(kernel, n_tm, n_rows),
        out_shape=jax.ShapeDtypeStruct((frames * 2 * rows, 2 * width * outputs), BF16),
        in_specs=[vmem, vmem, vmem, vmem, hbm, hbm],
        out_specs=vmem,
        scratch_shapes=[
            pltpu.VMEM(conv_first.shape, BF16),
            pltpu.VMEM((taps * LANES, chans), BF16),
            pltpu.VMEM((9, outputs, chans), BF16),
            pltpu.VMEM((n_tm, frames, rows, width, LANES), BF16),
            pltpu.VMEM((all_frames, rows + 2, width, LANES), BF16),
            pltpu.VMEM((3, all_frames + 2, rows + 2, width, LANES), BF16),
            pltpu.VMEM((n_tm, frames, rows, width, chans), BF16),
            pltpu.VMEM((n_tm, frames, rows, width, chans), BF16),
            pltpu.VMEM((2, frames, rows, width, chans), F32),
            pltpu.VMEM((frames, depth, width, chans), BF16),
            pltpu.VMEM((6 * cells, frames * depth * width), BF16),
            dma((2,)),
            dma((3 * n_tm,)),
            dma((3 * n_tm,)),
            dma((2 * n_tm,)),
            dma((2 * n_tm,)),
            dma((2,)),
            dma((2,)),
        ],
        compiler_params=pltpu.CompilerParams(
            collective_id=0, has_side_effects=True, vmem_limit_bytes=53 * 1024 * 1024
        ),
        cost_estimate=pl.CostEstimate(
            flops=flops, bytes_accessed=4 * 1024 * 1024, transcendentals=cells * chans
        ),
    )(
        latent,
        gain_first,
        bias_first,
        bias_upper,
        conv_first,
        jnp.swapaxes(conv_upper, 1, 2),
    )
    return decoded.reshape(frames, 2 * rows, 2 * width * outputs)


def solution(mesh):
    in_specs = (P("tm", "rows", None, None), P(), P(None, "tm", None), P(), P(), P())
    out_specs = P("tm", "rows", None)
    body = functools.partial(local, mesh.shape["tm"], mesh.shape["rows"])
    return jax.shard_map(body, mesh=mesh, in_specs=in_specs, out_specs=out_specs, check_vma=False)
```

```python
import functools

import jax
import jax.numpy as jnp
from jax import lax
from jax.experimental import pallas as pl
from jax.experimental.pallas import tpu as pltpu
from jax.sharding import PartitionSpec as P

MESH = pl.DeviceIdType.MESH
F32 = jnp.float32
BF16 = jnp.bfloat16
LANES = 128


def kernel(
    n_tm,
    n_rows,
    latent_hbm,
    gain_hbm,
    bias1_hbm,
    bias2_hbm,
    w1_hbm,
    wu_hbm,
    out_ref,
    latent_ref,
    gain_ref,
    bias1_ref,
    bias2_ref,
    w1_ref,
    wpad,
    wu_ref,
    send,
    recv,
    shifted,
    part_send,
    part_recv,
    own,
    block,
    pick,
    load_sem,
    act_send_sem,
    act_recv_sem,
    part_send_sem,
    part_recv_sem,
    row_send_sem,
    row_recv_sem,
):
    frames, rows, width, chans = latent_ref.shape
    cells = frames * rows * width
    taps, piece, _ = w1_ref.shape
    outputs = wu_ref.shape[1]
    me = lax.axis_index("tm")
    band = lax.axis_index("rows")
    above = lax.rem(band + n_rows - 1, n_rows)
    below = lax.rem(band + 1, n_rows)
    has_above = band > 0
    has_below = band < n_rows - 1

    load_latent = pltpu.make_async_copy(latent_hbm, latent_ref, load_sem.at[0])
    load_gain = pltpu.make_async_copy(gain_hbm, gain_ref, load_sem.at[1])
    load_w1 = pltpu.make_async_copy(w1_hbm, w1_ref, load_sem.at[2])
    load_bias1 = pltpu.make_async_copy(bias1_hbm, bias1_ref, load_sem.at[3])
    load_wu = pltpu.make_async_copy(wu_hbm, wu_ref, load_sem.at[4])
    load_bias2 = pltpu.make_async_copy(bias2_hbm, bias2_ref, load_sem.at[5])
    for load in (load_latent, load_gain, load_w1, load_bias1, load_wu, load_bias2):
        load.start()

    barrier = pltpu.get_barrier_semaphore()
    for d in range(1, n_tm):
        pl.semaphore_signal(
            barrier, inc=1, device_id=(lax.rem(me + d, n_tm), band), device_id_type=MESH
        )

    @pl.when(has_above)
    def _():
        for s in range(n_tm):
            pl.semaphore_signal(barrier, inc=1, device_id=(s, above), device_id_type=MESH)

    @pl.when(has_below)
    def _():
        for s in range(n_tm):
            pl.semaphore_signal(barrier, inc=1, device_id=(s, below), device_id_type=MESH)

    load_latent.wait()
    load_gain.wait()
    values = latent_ref[...].astype(F32).reshape(cells, chans)
    mean_square = jnp.mean(values * values, axis=-1, keepdims=True)
    scaled = values * lax.rsqrt(mean_square + 1e-06) * gain_ref[...].reshape(1, chans)
    act = scaled / (1.0 + jnp.exp(-scaled))
    blank = jnp.zeros((cells, LANES - piece), F32)
    for s in range(n_tm):
        cut = jnp.concatenate([act[:, s * piece : (s + 1) * piece], blank], axis=1)
        send[s] = cut.astype(BF16).reshape(frames, rows, width, LANES)

    neighbours = jnp.where(has_above, n_tm, 0) + jnp.where(has_below, n_tm, 0)
    pl.semaphore_wait(barrier, n_tm - 1 + neighbours)

    mine = pl.ds(me * frames, frames)

    def act_copy(s, kind, row, where, to):
        return pltpu.make_async_remote_copy(
            src_ref=send.at[s, :, row],
            dst_ref=recv.at[mine, where],
            send_sem=act_send_sem.at[3 * s + kind],
            recv_sem=act_recv_sem.at[3 * me + kind],
            device_id=(s, to),
            device_id_type=MESH,
        )

    def main_copy(s):
        return act_copy(s, 0, pl.ds(0, rows), pl.ds(1, rows), band)

    def down_copy(s):
        return act_copy(s, 1, pl.ds(rows - 1, 1), pl.ds(0, 1), below)

    def up_copy(s):
        return act_copy(s, 2, pl.ds(0, 1), pl.ds(rows + 1, 1), above)

    for d in range(1, n_tm):
        main_copy(lax.rem(me + d, n_tm)).start()

    @pl.when(has_below)
    def _():
        for s in range(n_tm):
            down_copy(s).start()

    @pl.when(has_above)
    def _():
        for s in range(n_tm):
            up_copy(s).start()

    recv[mine, pl.ds(1, rows)] = send[me]
    all_frames = n_tm * frames
    edge = jnp.zeros((all_frames, 1, width, LANES), BF16)
    block_edge = jnp.zeros((frames, 1, width, chans), BF16)

    @pl.when(band == 0)
    def _():
        recv[:, pl.ds(0, 1)] = edge
        block[:, pl.ds(0, 1)] = block_edge

    @pl.when(band == n_rows - 1)
    def _():
        recv[:, pl.ds(rows + 1, 1)] = edge
        block[:, pl.ds(rows + 1, 1)] = block_edge

    shifted[:, pl.ds(0, 2)] = jnp.zeros((3, 2, rows + 2, width, LANES), BF16)

    big = 2 * rows
    depth = block.shape[1]
    block[:, pl.ds(rows + 2, depth - rows - 2)] = jnp.zeros(
        (frames, depth - rows - 2, width, chans), BF16
    )
    at = lax.broadcasted_iota(jnp.int32, (pick.shape[0], 1), 0)
    to = lax.broadcasted_iota(jnp.int32, pick.shape, 1)
    row_tap = at // (frames * width * big)
    col = (at // (frames * big)) % width
    frame = (at // big) % frames
    line = at % big
    source = frame * (depth * width) + ((line + row_tap + 1) // 2) * width + col
    pick[...] = jnp.where(to == source, 1.0, 0.0).astype(BF16)

    load_w1.wait()
    spare = jnp.zeros((LANES - piece, chans), BF16)
    for tap in range(taps):
        wpad[pl.ds(tap * LANES, LANES)] = jnp.concatenate([w1_ref[tap], spare], axis=0)

    def act_arrival(s, kind, row, where):
        return pltpu.make_async_remote_copy(
            src_ref=send.at[s, :, row],
            dst_ref=recv.at[pl.ds(s * frames, frames), where],
            send_sem=act_send_sem.at[3 * s + kind],
            recv_sem=act_recv_sem.at[3 * s + kind],
            device_id=(lax.rem(me + 1, n_tm), band),
            device_id_type=MESH,
        )

    for d in range(1, n_tm):
        s = lax.rem(me + d, n_tm)
        act_arrival(s, 0, pl.ds(0, rows), pl.ds(1, rows)).wait_recv()

    @pl.when(has_above)
    def _():
        for s in range(n_tm):
            act_arrival(s, 1, pl.ds(0, 1), pl.ds(0, 1)).wait_recv()

    @pl.when(has_below)
    def _():
        for s in range(n_tm):
            act_arrival(s, 2, pl.ds(0, 1), pl.ds(rows + 1, 1)).wait_recv()

    tall = all_frames * (rows + 2) * width
    flat = recv[...].astype(F32).reshape(tall, LANES)
    column = lax.broadcasted_iota(jnp.int32, (tall, LANES), 0) % width
    left = jnp.where(column == 0, 0.0, pltpu.roll(flat, 1, 0))
    right = jnp.where(column == width - 1, 0.0, pltpu.roll(flat, tall - 1, 0))
    shape = (all_frames, rows + 2, width, LANES)
    shifted[0, pl.ds(2, all_frames)] = left.astype(BF16).reshape(shape)
    shifted[1, pl.ds(2, all_frames)] = recv[...]
    shifted[2, pl.ds(2, all_frames)] = right.astype(BF16).reshape(shape)

    pairs = n_tm // 2

    order = [0, rows - 1] + list(range(1, rows - 1))
    spans = (pl.ds(0, 2), pl.ds(2, rows - 2))

    def part_copy(s, kind):
        return pltpu.make_async_remote_copy(
            src_ref=part_send.at[s, :, spans[kind]],
            dst_ref=part_recv.at[me, :, spans[kind]],
            send_sem=part_send_sem.at[2 * s + kind],
            recv_sem=part_recv_sem.at[2 * me + kind],
            device_id=(s, band),
            device_id_type=MESH,
        )

    def part_arrival(s, kind):
        return pltpu.make_async_remote_copy(
            src_ref=part_send.at[s, :, spans[kind]],
            dst_ref=part_recv.at[s, :, spans[kind]],
            send_sem=part_send_sem.at[2 * s + kind],
            recv_sem=part_recv_sem.at[2 * s + kind],
            device_id=(s, band),
            device_id_type=MESH,
        )

    def stage(s, sums):
        for slot, row in enumerate(order):
            part_send[s, :, slot] = sums[:, row].astype(BF16)

    for k in range(1, pairs + 1):
        pair = lax.rem(lax.div(me, 2) + k, pairs)
        total = jnp.zeros((2 * cells, chans), F32)
        for dt in range(3):
            windows = []
            for dy in range(3):
                for dx in range(3):
                    start = pair * (2 * frames) + dt
                    view = shifted[dx, pl.ds(start, 2 * frames), pl.ds(dy, rows)]
                    windows.append(view.reshape(2 * cells, LANES))
            total = total + jnp.dot(
                jnp.concatenate(windows, axis=1),
                wpad[pl.ds(dt * 9 * LANES, 9 * LANES)],
                preferred_element_type=F32,
            )
        sums = total.reshape(2, frames, rows, width, chans)
        if k < pairs:
            for c in range(2):
                stage(2 * pair + c, sums[c])
            for kind in range(2):
                for c in range(2):
                    part_copy(2 * pair + c, kind).start()
        else:
            own[...] = sums
            mate = 2 * lax.div(me, 2) + (1 - lax.rem(me, 2))
            stage(mate, own[1 - lax.rem(me, 2)])
            for kind in range(2):
                part_copy(mate, kind).start()

    load_bias1.wait()
    bias1 = bias1_ref[...].reshape(1, 1, chans)

    def finish(kind):
        for d in range(1, n_tm):
            part_arrival(lax.rem(me + n_tm - d, n_tm), kind).wait_recv()
        for slot, row in enumerate(order):
            if (slot >= 2) != (kind == 1):
                continue
            summed = own[lax.rem(me, 2), :, row] + bias1 + latent_ref[:, row].astype(F32)
            for d in range(1, n_tm):
                summed = summed + part_recv[lax.rem(me + n_tm - d, n_tm), :, slot].astype(F32)
            block[:, row + 1] = summed.astype(BF16)

    finish(0)

    def row_copy(kind, row, where, to):
        return pltpu.make_async_remote_copy(
            src_ref=block.at[:, pl.ds(row, 1)],
            dst_ref=block.at[:, pl.ds(where, 1)],
            send_sem=row_send_sem.at[kind],
            recv_sem=row_recv_sem.at[kind],
            device_id=(me, to),
            device_id_type=MESH,
        )

    @pl.when(has_below)
    def _():
        row_copy(0, rows, 0, below).start()

    @pl.when(has_above)
    def _():
        row_copy(1, 1, rows + 1, above).start()

    finish(1)
    load_wu.wait()
    load_bias2.wait()

    @pl.when(has_above)
    def _():
        row_copy(0, rows, 0, above).wait_recv()

    @pl.when(has_below)
    def _():
        row_copy(1, 1, rows + 1, below).wait_recv()

    spread = jnp.dot(
        pick[...],
        block[...].reshape(frames * depth * width, chans),
        preferred_element_type=F32,
    ).astype(BF16)
    high = frames * width * big
    lines = jnp.concatenate([spread[k * high : (k + 1) * high] for k in range(3)], axis=1)
    cols = []
    for dx in range(3):
        weights = jnp.concatenate([wu_ref[dx], wu_ref[3 + dx], wu_ref[6 + dx]], axis=1)
        product = lax.dot_general(
            lines, weights, (((1,), (1,)), ((), ())), preferred_element_type=F32
        )
        cols.append(product.reshape(width, frames * big, outputs))
    nothing = jnp.zeros((1, frames * big, outputs), F32)
    before = jnp.concatenate([nothing, cols[0][: width - 1]], axis=0)
    after = jnp.concatenate([cols[2][1:], nothing], axis=0)
    bias2 = bias2_ref[...].reshape(1, 1, outputs)
    even = before + cols[1] + cols[2] + bias2
    odd = cols[0] + cols[1] + after + bias2
    both = jnp.concatenate([even, odd], axis=-1).astype(BF16)
    for c in range(width):
        out_ref[:, pl.ds(c * 2 * outputs, 2 * outputs)] = both[c]

    for d in range(1, n_tm):
        s = lax.rem(me + d, n_tm)
        main_copy(s).wait_send()
        for kind in range(2):
            part_copy(s, kind).wait_send()

    @pl.when(has_below)
    def _():
        for s in range(n_tm):
            down_copy(s).wait_send()
        row_copy(0, rows, 0, below).wait_send()

    @pl.when(has_above)
    def _():
        for s in range(n_tm):
            up_copy(s).wait_send()
        row_copy(1, 1, rows + 1, above).wait_send()


def local(n_tm, n_rows, latent, gain_first, conv_first, bias_first, conv_upper, bias_upper):
    frames, rows, width, chans = latent.shape
    outputs = conv_upper.shape[2]
    taps, piece, _ = conv_first.shape
    cells = frames * rows * width
    all_frames = n_tm * frames
    depth = rows + 4
    vmem = pl.BlockSpec(memory_space=pltpu.VMEM)
    hbm = pl.BlockSpec(memory_space=pl.ANY)
    dma = pltpu.SemaphoreType.DMA
    flops = 2 * taps * piece * chans * all_frames * rows * width + 18 * 4 * cells * chans * outputs
    decoded = pl.pallas_call(
        functools.partial(kernel, n_tm, n_rows),
        out_shape=jax.ShapeDtypeStruct((frames * 2 * rows, 2 * width * outputs), BF16),
        in_specs=[hbm] * 6,
        out_specs=vmem,
        scratch_shapes=[
            pltpu.VMEM(latent.shape, BF16),
            pltpu.VMEM((chans,), F32),
            pltpu.VMEM((chans,), F32),
            pltpu.VMEM((outputs,), F32),
            pltpu.VMEM(conv_first.shape, BF16),
            pltpu.VMEM((taps * LANES, chans), BF16),
            pltpu.VMEM((9, outputs, chans), BF16),
            pltpu.VMEM((n_tm, frames, rows, width, LANES), BF16),
            pltpu.VMEM((all_frames, rows + 2, width, LANES), BF16),
            pltpu.VMEM((3, all_frames + 2, rows + 2, width, LANES), BF16),
            pltpu.VMEM((n_tm, frames, rows, width, chans), BF16),
            pltpu.VMEM((n_tm, frames, rows, width, chans), BF16),
            pltpu.VMEM((2, frames, rows, width, chans), F32),
            pltpu.VMEM((frames, depth, width, chans), BF16),
            pltpu.VMEM((6 * cells, frames * depth * width), BF16),
            dma((6,)),
            dma((3 * n_tm,)),
            dma((3 * n_tm,)),
            dma((2 * n_tm,)),
            dma((2 * n_tm,)),
            dma((2,)),
            dma((2,)),
        ],
        compiler_params=pltpu.CompilerParams(
            collective_id=0, has_side_effects=True, vmem_limit_bytes=60 * 1024 * 1024
        ),
        cost_estimate=pl.CostEstimate(
            flops=flops, bytes_accessed=4 * 1024 * 1024, transcendentals=cells * chans
        ),
    )(
        latent,
        gain_first,
        bias_first,
        bias_upper,
        conv_first,
        jnp.swapaxes(conv_upper, 1, 2),
    )
    return decoded.reshape(frames, 2 * rows, 2 * width * outputs)


def solution(mesh):
    in_specs = (P("tm", "rows", None, None), P(), P(None, "tm", None), P(), P(), P())
    out_specs = P("tm", "rows", None)
    body = functools.partial(local, mesh.shape["tm"], mesh.shape["rows"])
    return jax.shard_map(body, mesh=mesh, in_specs=in_specs, out_specs=out_specs, check_vma=False)
```

```python
import functools

import jax
import jax.numpy as jnp
from jax import lax
from jax.experimental import pallas as pl
from jax.experimental.pallas import tpu as pltpu
from jax.sharding import PartitionSpec as P

MESH = pl.DeviceIdType.MESH
F32 = jnp.float32
BF16 = jnp.bfloat16
LANES = 128


def quotient(number, by):
    if by & (by - 1):
        return number // by
    return lax.shift_right_logical(number, by.bit_length() - 1)


def remainder(number, by):
    return number % by if by & (by - 1) else number & (by - 1)


def kernel(
    n_tm,
    n_rows,
    latent_hbm,
    gain_hbm,
    bias1_hbm,
    bias2_hbm,
    w1_hbm,
    wu_hbm,
    out_ref,
    latent_ref,
    gain_ref,
    bias1_ref,
    bias2_ref,
    w1_ref,
    wpad,
    wu_ref,
    send,
    recv,
    shifted,
    part_send,
    part_recv,
    own,
    block,
    pick,
    load_sem,
    act_send_sem,
    act_recv_sem,
    part_send_sem,
    part_recv_sem,
    row_send_sem,
    row_recv_sem,
):
    frames, rows, width, chans = latent_ref.shape
    cells = frames * rows * width
    taps, piece, _ = w1_ref.shape
    outputs = wu_ref.shape[1]
    me = lax.axis_index("tm")
    band = lax.axis_index("rows")
    above = lax.rem(band + n_rows - 1, n_rows)
    below = lax.rem(band + 1, n_rows)
    has_above = band > 0
    has_below = band < n_rows - 1

    load_latent = pltpu.make_async_copy(latent_hbm, latent_ref, load_sem.at[0])
    load_gain = pltpu.make_async_copy(gain_hbm, gain_ref, load_sem.at[1])
    load_w1 = pltpu.make_async_copy(w1_hbm, w1_ref, load_sem.at[2])
    load_bias1 = pltpu.make_async_copy(bias1_hbm, bias1_ref, load_sem.at[3])
    load_wu = pltpu.make_async_copy(wu_hbm, wu_ref, load_sem.at[4])
    load_bias2 = pltpu.make_async_copy(bias2_hbm, bias2_ref, load_sem.at[5])
    for load in (load_latent, load_gain, load_w1, load_bias1, load_wu, load_bias2):
        load.start()

    barrier = pltpu.get_barrier_semaphore()
    for d in range(1, n_tm):
        pl.semaphore_signal(
            barrier, inc=1, device_id=(lax.rem(me + d, n_tm), band), device_id_type=MESH
        )

    @pl.when(has_above)
    def _():
        for s in range(n_tm):
            pl.semaphore_signal(barrier, inc=1, device_id=(s, above), device_id_type=MESH)

    @pl.when(has_below)
    def _():
        for s in range(n_tm):
            pl.semaphore_signal(barrier, inc=1, device_id=(s, below), device_id_type=MESH)

    load_latent.wait()
    load_gain.wait()
    values = latent_ref[...].astype(F32).reshape(cells, chans)
    mean_square = jnp.mean(values * values, axis=-1, keepdims=True)
    scaled = values * lax.rsqrt(mean_square + 1e-06) * gain_ref[...].reshape(1, chans)
    act = scaled / (1.0 + jnp.exp(-scaled))
    blank = jnp.zeros((cells, LANES - piece), F32)
    for s in range(n_tm):
        cut = jnp.concatenate([act[:, s * piece : (s + 1) * piece], blank], axis=1)
        send[s] = cut.astype(BF16).reshape(frames, rows, width, LANES)

    neighbours = jnp.where(has_above, n_tm, 0) + jnp.where(has_below, n_tm, 0)
    pl.semaphore_wait(barrier, n_tm - 1 + neighbours)

    mine = pl.ds(me * frames, frames)

    def act_copy(s, kind, row, where, to):
        return pltpu.make_async_remote_copy(
            src_ref=send.at[s, :, row],
            dst_ref=recv.at[mine, where],
            send_sem=act_send_sem.at[3 * s + kind],
            recv_sem=act_recv_sem.at[3 * me + kind],
            device_id=(s, to),
            device_id_type=MESH,
        )

    def main_copy(s):
        return act_copy(s, 0, pl.ds(0, rows), pl.ds(1, rows), band)

    def down_copy(s):
        return act_copy(s, 1, pl.ds(rows - 1, 1), pl.ds(0, 1), below)

    def up_copy(s):
        return act_copy(s, 2, pl.ds(0, 1), pl.ds(rows + 1, 1), above)

    for d in range(1, n_tm):
        main_copy(lax.rem(me + d, n_tm)).start()

    @pl.when(has_below)
    def _():
        for s in range(n_tm):
            down_copy(s).start()

    @pl.when(has_above)
    def _():
        for s in range(n_tm):
            up_copy(s).start()

    recv[mine, pl.ds(1, rows)] = send[me]
    all_frames = n_tm * frames
    edge = jnp.zeros((all_frames, 1, width, LANES), BF16)
    block_edge = jnp.zeros((frames, 1, width, chans), BF16)

    @pl.when(band == 0)
    def _():
        recv[:, pl.ds(0, 1)] = edge
        block[:, pl.ds(0, 1)] = block_edge

    @pl.when(band == n_rows - 1)
    def _():
        recv[:, pl.ds(rows + 1, 1)] = edge
        block[:, pl.ds(rows + 1, 1)] = block_edge

    shifted[:, pl.ds(0, 2)] = jnp.zeros((3, 2, rows + 2, width, LANES), BF16)

    big = 2 * rows
    depth = block.shape[1]
    block[:, pl.ds(rows + 2, depth - rows - 2)] = jnp.zeros(
        (frames, depth - rows - 2, width, chans), BF16
    )
    load_w1.wait()
    spare = jnp.zeros((LANES - piece, chans), BF16)
    for tap in range(taps):
        wpad[pl.ds(tap * LANES, LANES)] = jnp.concatenate([w1_ref[tap], spare], axis=0)

    def act_arrival(s, kind, row, where):
        return pltpu.make_async_remote_copy(
            src_ref=send.at[s, :, row],
            dst_ref=recv.at[pl.ds(s * frames, frames), where],
            send_sem=act_send_sem.at[3 * s + kind],
            recv_sem=act_recv_sem.at[3 * s + kind],
            device_id=(lax.rem(me + 1, n_tm), band),
            device_id_type=MESH,
        )

    for d in range(1, n_tm):
        s = lax.rem(me + d, n_tm)
        act_arrival(s, 0, pl.ds(0, rows), pl.ds(1, rows)).wait_recv()

    @pl.when(has_above)
    def _():
        for s in range(n_tm):
            act_arrival(s, 1, pl.ds(0, 1), pl.ds(0, 1)).wait_recv()

    @pl.when(has_below)
    def _():
        for s in range(n_tm):
            act_arrival(s, 2, pl.ds(0, 1), pl.ds(rows + 1, 1)).wait_recv()

    tall = all_frames * (rows + 2) * width
    flat = recv[...].astype(F32).reshape(tall, LANES)
    column = remainder(lax.broadcasted_iota(jnp.int32, (tall, LANES), 0), width)
    left = jnp.where(column == 0, 0.0, pltpu.roll(flat, 1, 0))
    right = jnp.where(column == width - 1, 0.0, pltpu.roll(flat, tall - 1, 0))
    shape = (all_frames, rows + 2, width, LANES)
    shifted[0, pl.ds(2, all_frames)] = left.astype(BF16).reshape(shape)
    shifted[1, pl.ds(2, all_frames)] = recv[...]
    shifted[2, pl.ds(2, all_frames)] = right.astype(BF16).reshape(shape)

    pairs = n_tm // 2

    order = [0, rows - 1] + list(range(1, rows - 1))
    spans = (pl.ds(0, 2), pl.ds(2, rows - 2))

    def part_copy(s, kind):
        return pltpu.make_async_remote_copy(
            src_ref=part_send.at[s, :, spans[kind]],
            dst_ref=part_recv.at[me, :, spans[kind]],
            send_sem=part_send_sem.at[2 * s + kind],
            recv_sem=part_recv_sem.at[2 * me + kind],
            device_id=(s, band),
            device_id_type=MESH,
        )

    def part_arrival(s, kind):
        return pltpu.make_async_remote_copy(
            src_ref=part_send.at[s, :, spans[kind]],
            dst_ref=part_recv.at[s, :, spans[kind]],
            send_sem=part_send_sem.at[2 * s + kind],
            recv_sem=part_recv_sem.at[2 * s + kind],
            device_id=(s, band),
            device_id_type=MESH,
        )

    def stage(s, sums):
        for slot, row in enumerate(order):
            part_send[s, :, slot] = sums[:, row].astype(BF16)

    for k in range(1, pairs + 1):
        pair = lax.rem(lax.div(me, 2) + k, pairs)
        total = jnp.zeros((2 * cells, chans), F32)
        for dt in range(3):
            windows = []
            for dy in range(3):
                for dx in range(3):
                    start = pair * (2 * frames) + dt
                    view = shifted[dx, pl.ds(start, 2 * frames), pl.ds(dy, rows)]
                    windows.append(view.reshape(2 * cells, LANES))
            total = total + jnp.dot(
                jnp.concatenate(windows, axis=1),
                wpad[pl.ds(dt * 9 * LANES, 9 * LANES)],
                preferred_element_type=F32,
            )
        sums = total.reshape(2, frames, rows, width, chans)
        if k < pairs:
            for c in range(2):
                stage(2 * pair + c, sums[c])
            for kind in range(2):
                for c in range(2):
                    part_copy(2 * pair + c, kind).start()
        else:
            own[...] = sums
            mate = 2 * lax.div(me, 2) + (1 - lax.rem(me, 2))
            stage(mate, own[1 - lax.rem(me, 2)])
            for kind in range(2):
                part_copy(mate, kind).start()

    at = lax.broadcasted_iota(jnp.int32, (pick.shape[0], 1), 0)
    to = lax.broadcasted_iota(jnp.int32, pick.shape, 1)
    row_tap = quotient(at, frames * width * big)
    col = remainder(quotient(at, frames * big), width)
    frame = remainder(quotient(at, big), frames)
    line = remainder(at, big)
    source = frame * (depth * width) + quotient(line + row_tap + 1, 2) * width + col
    pick[...] = jnp.where(to == source, 1.0, 0.0).astype(BF16)

    load_bias1.wait()
    bias1 = bias1_ref[...].reshape(1, 1, chans)

    def finish(kind):
        for d in range(1, n_tm):
            part_arrival(lax.rem(me + n_tm - d, n_tm), kind).wait_recv()
        for slot, row in enumerate(order):
            if (slot >= 2) != (kind == 1):
                continue
            summed = own[lax.rem(me, 2), :, row] + bias1 + latent_ref[:, row].astype(F32)
            for d in range(1, n_tm):
                summed = summed + part_recv[lax.rem(me + n_tm - d, n_tm), :, slot].astype(F32)
            block[:, row + 1] = summed.astype(BF16)

    finish(0)

    def row_copy(kind, row, where, to):
        return pltpu.make_async_remote_copy(
            src_ref=block.at[:, pl.ds(row, 1)],
            dst_ref=block.at[:, pl.ds(where, 1)],
            send_sem=row_send_sem.at[kind],
            recv_sem=row_recv_sem.at[kind],
            device_id=(me, to),
            device_id_type=MESH,
        )

    @pl.when(has_below)
    def _():
        row_copy(0, rows, 0, below).start()

    @pl.when(has_above)
    def _():
        row_copy(1, 1, rows + 1, above).start()

    finish(1)
    load_wu.wait()
    load_bias2.wait()

    @pl.when(has_above)
    def _():
        row_copy(0, rows, 0, above).wait_recv()

    @pl.when(has_below)
    def _():
        row_copy(1, 1, rows + 1, below).wait_recv()

    spread = jnp.dot(
        pick[...],
        block[...].reshape(frames * depth * width, chans),
        preferred_element_type=F32,
    ).astype(BF16)
    high = frames * width * big
    lines = jnp.concatenate([spread[k * high : (k + 1) * high] for k in range(3)], axis=1)
    cols = []
    for dx in range(3):
        weights = jnp.concatenate([wu_ref[dx], wu_ref[3 + dx], wu_ref[6 + dx]], axis=1)
        product = lax.dot_general(
            lines, weights, (((1,), (1,)), ((), ())), preferred_element_type=F32
        )
        cols.append(product.reshape(width, frames * big, outputs))
    nothing = jnp.zeros((1, frames * big, outputs), F32)
    before = jnp.concatenate([nothing, cols[0][: width - 1]], axis=0)
    after = jnp.concatenate([cols[2][1:], nothing], axis=0)
    bias2 = bias2_ref[...].reshape(1, 1, outputs)
    even = before + cols[1] + cols[2] + bias2
    odd = cols[0] + cols[1] + after + bias2
    both = jnp.concatenate([even, odd], axis=-1).astype(BF16)
    for c in range(width):
        out_ref[:, pl.ds(c * 2 * outputs, 2 * outputs)] = both[c]

    for d in range(1, n_tm):
        s = lax.rem(me + d, n_tm)
        main_copy(s).wait_send()
        for kind in range(2):
            part_copy(s, kind).wait_send()

    @pl.when(has_below)
    def _():
        for s in range(n_tm):
            down_copy(s).wait_send()
        row_copy(0, rows, 0, below).wait_send()

    @pl.when(has_above)
    def _():
        for s in range(n_tm):
            up_copy(s).wait_send()
        row_copy(1, 1, rows + 1, above).wait_send()


def local(n_tm, n_rows, latent, gain_first, conv_first, bias_first, conv_upper, bias_upper):
    frames, rows, width, chans = latent.shape
    outputs = conv_upper.shape[2]
    taps, piece, _ = conv_first.shape
    cells = frames * rows * width
    all_frames = n_tm * frames
    depth = rows + 4
    vmem = pl.BlockSpec(memory_space=pltpu.VMEM)
    hbm = pl.BlockSpec(memory_space=pl.ANY)
    dma = pltpu.SemaphoreType.DMA
    flops = 2 * taps * piece * chans * all_frames * rows * width + 18 * 4 * cells * chans * outputs
    decoded = pl.pallas_call(
        functools.partial(kernel, n_tm, n_rows),
        out_shape=jax.ShapeDtypeStruct((frames * 2 * rows, 2 * width * outputs), BF16),
        in_specs=[hbm] * 6,
        out_specs=vmem,
        scratch_shapes=[
            pltpu.VMEM(latent.shape, BF16),
            pltpu.VMEM((chans,), F32),
            pltpu.VMEM((chans,), F32),
            pltpu.VMEM((outputs,), F32),
            pltpu.VMEM(conv_first.shape, BF16),
            pltpu.VMEM((taps * LANES, chans), BF16),
            pltpu.VMEM((9, outputs, chans), BF16),
            pltpu.VMEM((n_tm, frames, rows, width, LANES), BF16),
            pltpu.VMEM((all_frames, rows + 2, width, LANES), BF16),
            pltpu.VMEM((3, all_frames + 2, rows + 2, width, LANES), BF16),
            pltpu.VMEM((n_tm, frames, rows, width, chans), BF16),
            pltpu.VMEM((n_tm, frames, rows, width, chans), BF16),
            pltpu.VMEM((2, frames, rows, width, chans), F32),
            pltpu.VMEM((frames, depth, width, chans), BF16),
            pltpu.VMEM((6 * cells, frames * depth * width), BF16),
            dma((6,)),
            dma((3 * n_tm,)),
            dma((3 * n_tm,)),
            dma((2 * n_tm,)),
            dma((2 * n_tm,)),
            dma((2,)),
            dma((2,)),
        ],
        compiler_params=pltpu.CompilerParams(
            collective_id=0, has_side_effects=True, vmem_limit_bytes=60 * 1024 * 1024
        ),
        cost_estimate=pl.CostEstimate(
            flops=flops, bytes_accessed=4 * 1024 * 1024, transcendentals=cells * chans
        ),
    )(
        latent,
        gain_first,
        bias_first,
        bias_upper,
        conv_first,
        jnp.swapaxes(conv_upper, 1, 2),
    )
    return decoded.reshape(frames, 2 * rows, 2 * width * outputs)


def solution(mesh):
    in_specs = (P("tm", "rows", None, None), P(), P(None, "tm", None), P(), P(), P())
    out_specs = P("tm", "rows", None)
    body = functools.partial(local, mesh.shape["tm"], mesh.shape["rows"])
    return jax.shard_map(body, mesh=mesh, in_specs=in_specs, out_specs=out_specs, check_vma=False)
```

```python
import functools

import jax
import jax.numpy as jnp
from jax import lax
from jax.experimental import pallas as pl
from jax.experimental.pallas import tpu as pltpu
from jax.sharding import PartitionSpec as P

MESH = pl.DeviceIdType.MESH
F32 = jnp.float32
BF16 = jnp.bfloat16
LANES = 128


def quotient(number, by):
    if by & (by - 1):
        return number // by
    return lax.shift_right_logical(number, by.bit_length() - 1)


def remainder(number, by):
    return number % by if by & (by - 1) else number & (by - 1)


def kernel(
    n_tm,
    n_rows,
    latent_hbm,
    gain_hbm,
    bias1_hbm,
    bias2_hbm,
    w1_hbm,
    wu_hbm,
    out_ref,
    latent_ref,
    gain_ref,
    bias1_ref,
    bias2_ref,
    w1_ref,
    wpad,
    wu_ref,
    send,
    recv,
    shifted,
    part_send,
    part_recv,
    relay_send,
    relay_recv,
    held,
    own,
    block,
    pick,
    load_sem,
    act_send_sem,
    act_recv_sem,
    part_send_sem,
    part_recv_sem,
    relay_send_sem,
    relay_recv_sem,
    row_send_sem,
    row_recv_sem,
):
    frames, rows, width, chans = latent_ref.shape
    cells = frames * rows * width
    taps, piece, _ = w1_ref.shape
    outputs = wu_ref.shape[1]
    me = lax.axis_index("tm")
    band = lax.axis_index("rows")
    above = lax.rem(band + n_rows - 1, n_rows)
    below = lax.rem(band + 1, n_rows)
    has_above = band > 0
    has_below = band < n_rows - 1

    load_latent = pltpu.make_async_copy(latent_hbm, latent_ref, load_sem.at[0])
    load_gain = pltpu.make_async_copy(gain_hbm, gain_ref, load_sem.at[1])
    load_w1 = pltpu.make_async_copy(w1_hbm, w1_ref, load_sem.at[2])
    load_bias1 = pltpu.make_async_copy(bias1_hbm, bias1_ref, load_sem.at[3])
    load_wu = pltpu.make_async_copy(wu_hbm, wu_ref, load_sem.at[4])
    load_bias2 = pltpu.make_async_copy(bias2_hbm, bias2_ref, load_sem.at[5])
    for load in (load_latent, load_gain, load_w1, load_bias1, load_wu, load_bias2):
        load.start()

    barrier = pltpu.get_barrier_semaphore()
    for d in range(1, n_tm):
        pl.semaphore_signal(
            barrier, inc=1, device_id=(lax.rem(me + d, n_tm), band), device_id_type=MESH
        )

    @pl.when(has_above)
    def _():
        for s in range(n_tm):
            pl.semaphore_signal(barrier, inc=1, device_id=(s, above), device_id_type=MESH)

    @pl.when(has_below)
    def _():
        for s in range(n_tm):
            pl.semaphore_signal(barrier, inc=1, device_id=(s, below), device_id_type=MESH)

    load_latent.wait()
    load_gain.wait()
    values = latent_ref[...].astype(F32).reshape(cells, chans)
    mean_square = jnp.mean(values * values, axis=-1, keepdims=True)
    scaled = values * lax.rsqrt(mean_square + 1e-06) * gain_ref[...].reshape(1, chans)
    act = scaled / (1.0 + jnp.exp(-scaled))
    blank = jnp.zeros((cells, LANES - piece), F32)
    for s in range(n_tm):
        cut = jnp.concatenate([act[:, s * piece : (s + 1) * piece], blank], axis=1)
        send[s] = cut.astype(BF16).reshape(frames, rows, width, LANES)

    neighbours = jnp.where(has_above, n_tm, 0) + jnp.where(has_below, n_tm, 0)
    pl.semaphore_wait(barrier, n_tm - 1 + neighbours)

    mine = pl.ds(me * frames, frames)

    def act_copy(s, kind, row, where, to):
        return pltpu.make_async_remote_copy(
            src_ref=send.at[s, :, row],
            dst_ref=recv.at[mine, where],
            send_sem=act_send_sem.at[3 * s + kind],
            recv_sem=act_recv_sem.at[3 * me + kind],
            device_id=(s, to),
            device_id_type=MESH,
        )

    def main_copy(s):
        return act_copy(s, 0, pl.ds(0, rows), pl.ds(1, rows), band)

    def down_copy(s):
        return act_copy(s, 1, pl.ds(rows - 1, 1), pl.ds(0, 1), below)

    def up_copy(s):
        return act_copy(s, 2, pl.ds(0, 1), pl.ds(rows + 1, 1), above)

    for d in range(1, n_tm):
        main_copy(lax.rem(me + d, n_tm)).start()

    @pl.when(has_below)
    def _():
        for s in range(n_tm):
            down_copy(s).start()

    @pl.when(has_above)
    def _():
        for s in range(n_tm):
            up_copy(s).start()

    recv[mine, pl.ds(1, rows)] = send[me]
    all_frames = n_tm * frames
    edge = jnp.zeros((all_frames, 1, width, LANES), BF16)
    block_edge = jnp.zeros((frames, 1, width, chans), BF16)

    @pl.when(band == 0)
    def _():
        recv[:, pl.ds(0, 1)] = edge
        block[:, pl.ds(0, 1)] = block_edge

    @pl.when(band == n_rows - 1)
    def _():
        recv[:, pl.ds(rows + 1, 1)] = edge
        block[:, pl.ds(rows + 1, 1)] = block_edge

    shifted[:, pl.ds(0, 2)] = jnp.zeros((3, 2, rows + 2, width, LANES), BF16)

    big = 2 * rows
    depth = block.shape[1]
    block[:, pl.ds(rows + 2, depth - rows - 2)] = jnp.zeros(
        (frames, depth - rows - 2, width, chans), BF16
    )
    at = lax.broadcasted_iota(jnp.int32, (pick.shape[0], 1), 0)
    to = lax.broadcasted_iota(jnp.int32, pick.shape, 1)
    row_tap = quotient(at, frames * width * big)
    col = remainder(quotient(at, frames * big), width)
    frame = remainder(quotient(at, big), frames)
    line = remainder(at, big)
    source = frame * (depth * width) + quotient(line + row_tap + 1, 2) * width + col
    pick[...] = jnp.where(to == source, 1.0, 0.0).astype(BF16)

    load_w1.wait()
    spare = jnp.zeros((LANES - piece, chans), BF16)
    for tap in range(taps):
        wpad[pl.ds(tap * LANES, LANES)] = jnp.concatenate([w1_ref[tap], spare], axis=0)

    def act_arrival(s, kind, row, where):
        return pltpu.make_async_remote_copy(
            src_ref=send.at[s, :, row],
            dst_ref=recv.at[pl.ds(s * frames, frames), where],
            send_sem=act_send_sem.at[3 * s + kind],
            recv_sem=act_recv_sem.at[3 * s + kind],
            device_id=(lax.rem(me + 1, n_tm), band),
            device_id_type=MESH,
        )

    for d in range(1, n_tm):
        s = lax.rem(me + d, n_tm)
        act_arrival(s, 0, pl.ds(0, rows), pl.ds(1, rows)).wait_recv()

    @pl.when(has_above)
    def _():
        for s in range(n_tm):
            act_arrival(s, 1, pl.ds(0, 1), pl.ds(0, 1)).wait_recv()

    @pl.when(has_below)
    def _():
        for s in range(n_tm):
            act_arrival(s, 2, pl.ds(0, 1), pl.ds(rows + 1, 1)).wait_recv()

    tall = all_frames * (rows + 2) * width
    flat = recv[...].astype(F32).reshape(tall, LANES)
    column = remainder(lax.broadcasted_iota(jnp.int32, (tall, LANES), 0), width)
    left = jnp.where(column == 0, 0.0, pltpu.roll(flat, 1, 0))
    right = jnp.where(column == width - 1, 0.0, pltpu.roll(flat, tall - 1, 0))
    shape = (all_frames, rows + 2, width, LANES)
    shifted[0, pl.ds(2, all_frames)] = left.astype(BF16).reshape(shape)
    shifted[1, pl.ds(2, all_frames)] = recv[...]
    shifted[2, pl.ds(2, all_frames)] = right.astype(BF16).reshape(shape)

    pairs = n_tm // 2

    order = [0, rows - 1] + list(range(1, rows - 1))
    spans = (pl.ds(0, 2), pl.ds(2, rows - 2))

    def part_copy(s, kind):
        return pltpu.make_async_remote_copy(
            src_ref=part_send.at[s, :, spans[kind]],
            dst_ref=part_recv.at[me, :, spans[kind]],
            send_sem=part_send_sem.at[2 * s + kind],
            recv_sem=part_recv_sem.at[2 * me + kind],
            device_id=(s, band),
            device_id_type=MESH,
        )

    def part_arrival(s, kind):
        return pltpu.make_async_remote_copy(
            src_ref=part_send.at[s, :, spans[kind]],
            dst_ref=part_recv.at[s, :, spans[kind]],
            send_sem=part_send_sem.at[2 * s + kind],
            recv_sem=part_recv_sem.at[2 * s + kind],
            device_id=(s, band),
            device_id_type=MESH,
        )

    def stage(s, sums):
        for slot, row in enumerate(order):
            part_send[s, :, slot] = sums[:, row].astype(BF16)

    core = lax.rem(me, 2)
    mate = 2 * lax.div(me, 2) + (1 - core)
    elsewhere = [2 * lax.rem(lax.div(me, 2) + k, pairs) for k in range(1, pairs)]

    def partial(start, count):
        total = jnp.zeros((count * cells, chans), F32)
        for dt in range(3):
            windows = []
            for dy in range(3):
                for dx in range(3):
                    view = shifted[dx, pl.ds(start * frames + dt, count * frames), pl.ds(dy, rows)]
                    windows.append(view.reshape(count * cells, LANES))
            total = total + jnp.dot(
                jnp.concatenate(windows, axis=1),
                wpad[pl.ds(dt * 9 * LANES, 9 * LANES)],
                preferred_element_type=F32,
            )
        return total.reshape(count, frames, rows, width, chans)

    def relay(k):
        return pltpu.make_async_remote_copy(
            src_ref=relay_send.at[k],
            dst_ref=relay_recv.at[k],
            send_sem=relay_send_sem.at[k],
            recv_sem=relay_recv_sem.at[k],
            device_id=(mate, band),
            device_id_type=MESH,
        )

    for k, first in enumerate(elsewhere):
        relay_send[k] = partial(first + (1 - core), 1)[0].astype(BF16)
        relay(k).start()
        held[k] = partial(first + core, 1)[0]
    for k, first in enumerate(elsewhere):
        relay(k).wait_recv()
        stage(first + core, held[k] + relay_recv[k].astype(F32))
        for kind in range(2):
            part_copy(first + core, kind).start()
    own[...] = partial(2 * lax.div(me, 2), 2)
    stage(mate, own[1 - core])
    for kind in range(2):
        part_copy(mate, kind).start()

    sources = [mate] + [first + core for first in elsewhere]
    load_bias1.wait()
    bias1 = bias1_ref[...].reshape(1, 1, chans)

    def finish(kind):
        for s in sources:
            part_arrival(s, kind).wait_recv()
        for slot, row in enumerate(order):
            if (slot >= 2) != (kind == 1):
                continue
            summed = own[core, :, row] + bias1 + latent_ref[:, row].astype(F32)
            for s in sources:
                summed = summed + part_recv[s, :, slot].astype(F32)
            block[:, row + 1] = summed.astype(BF16)

    finish(0)

    def row_copy(kind, row, where, to):
        return pltpu.make_async_remote_copy(
            src_ref=block.at[:, pl.ds(row, 1)],
            dst_ref=block.at[:, pl.ds(where, 1)],
            send_sem=row_send_sem.at[kind],
            recv_sem=row_recv_sem.at[kind],
            device_id=(me, to),
            device_id_type=MESH,
        )

    @pl.when(has_below)
    def _():
        row_copy(0, rows, 0, below).start()

    @pl.when(has_above)
    def _():
        row_copy(1, 1, rows + 1, above).start()

    finish(1)
    load_wu.wait()
    load_bias2.wait()

    @pl.when(has_above)
    def _():
        row_copy(0, rows, 0, above).wait_recv()

    @pl.when(has_below)
    def _():
        row_copy(1, 1, rows + 1, below).wait_recv()

    spread = jnp.dot(
        pick[...],
        block[...].reshape(frames * depth * width, chans),
        preferred_element_type=F32,
    ).astype(BF16)
    high = frames * width * big
    lines = jnp.concatenate([spread[k * high : (k + 1) * high] for k in range(3)], axis=1)
    cols = []
    for dx in range(3):
        weights = jnp.concatenate([wu_ref[dx], wu_ref[3 + dx], wu_ref[6 + dx]], axis=1)
        product = lax.dot_general(
            lines, weights, (((1,), (1,)), ((), ())), preferred_element_type=F32
        )
        cols.append(product.reshape(width, frames * big, outputs))
    nothing = jnp.zeros((1, frames * big, outputs), F32)
    before = jnp.concatenate([nothing, cols[0][: width - 1]], axis=0)
    after = jnp.concatenate([cols[2][1:], nothing], axis=0)
    bias2 = bias2_ref[...].reshape(1, 1, outputs)
    even = before + cols[1] + cols[2] + bias2
    odd = cols[0] + cols[1] + after + bias2
    both = jnp.concatenate([even, odd], axis=-1).astype(BF16)
    for c in range(width):
        out_ref[:, pl.ds(c * 2 * outputs, 2 * outputs)] = both[c]

    for d in range(1, n_tm):
        s = lax.rem(me + d, n_tm)
        main_copy(s).wait_send()
    for s in sources:
        for kind in range(2):
            part_copy(s, kind).wait_send()
    for k in range(pairs - 1):
        relay(k).wait_send()

    @pl.when(has_below)
    def _():
        for s in range(n_tm):
            down_copy(s).wait_send()
        row_copy(0, rows, 0, below).wait_send()

    @pl.when(has_above)
    def _():
        for s in range(n_tm):
            up_copy(s).wait_send()
        row_copy(1, 1, rows + 1, above).wait_send()


def local(n_tm, n_rows, latent, gain_first, conv_first, bias_first, conv_upper, bias_upper):
    frames, rows, width, chans = latent.shape
    outputs = conv_upper.shape[2]
    taps, piece, _ = conv_first.shape
    cells = frames * rows * width
    all_frames = n_tm * frames
    depth = rows + 4
    others = n_tm // 2 - 1
    vmem = pl.BlockSpec(memory_space=pltpu.VMEM)
    hbm = pl.BlockSpec(memory_space=pl.ANY)
    dma = pltpu.SemaphoreType.DMA
    flops = 2 * taps * piece * chans * all_frames * rows * width + 18 * 4 * cells * chans * outputs
    decoded = pl.pallas_call(
        functools.partial(kernel, n_tm, n_rows),
        out_shape=jax.ShapeDtypeStruct((frames * 2 * rows, 2 * width * outputs), BF16),
        in_specs=[hbm] * 6,
        out_specs=vmem,
        scratch_shapes=[
            pltpu.VMEM(latent.shape, BF16),
            pltpu.VMEM((chans,), F32),
            pltpu.VMEM((chans,), F32),
            pltpu.VMEM((outputs,), F32),
            pltpu.VMEM(conv_first.shape, BF16),
            pltpu.VMEM((taps * LANES, chans), BF16),
            pltpu.VMEM((9, outputs, chans), BF16),
            pltpu.VMEM((n_tm, frames, rows, width, LANES), BF16),
            pltpu.VMEM((all_frames, rows + 2, width, LANES), BF16),
            pltpu.VMEM((3, all_frames + 2, rows + 2, width, LANES), BF16),
            pltpu.VMEM((n_tm, frames, rows, width, chans), BF16),
            pltpu.VMEM((n_tm, frames, rows, width, chans), BF16),
            pltpu.VMEM((others, frames, rows, width, chans), BF16),
            pltpu.VMEM((others, frames, rows, width, chans), BF16),
            pltpu.VMEM((others, frames, rows, width, chans), F32),
            pltpu.VMEM((2, frames, rows, width, chans), F32),
            pltpu.VMEM((frames, depth, width, chans), BF16),
            pltpu.VMEM((6 * cells, frames * depth * width), BF16),
            dma((6,)),
            dma((3 * n_tm,)),
            dma((3 * n_tm,)),
            dma((2 * n_tm,)),
            dma((2 * n_tm,)),
            dma((others,)),
            dma((others,)),
            dma((2,)),
            dma((2,)),
        ],
        compiler_params=pltpu.CompilerParams(
            collective_id=0, has_side_effects=True, vmem_limit_bytes=60 * 1024 * 1024
        ),
        cost_estimate=pl.CostEstimate(
            flops=flops, bytes_accessed=4 * 1024 * 1024, transcendentals=cells * chans
        ),
    )(
        latent,
        gain_first,
        bias_first,
        bias_upper,
        conv_first,
        jnp.swapaxes(conv_upper, 1, 2),
    )
    return decoded.reshape(frames, 2 * rows, 2 * width * outputs)


def solution(mesh):
    in_specs = (P("tm", "rows", None, None), P(), P(None, "tm", None), P(), P(), P())
    out_specs = P("tm", "rows", None)
    body = functools.partial(local, mesh.shape["tm"], mesh.shape["rows"])
    return jax.shard_map(body, mesh=mesh, in_specs=in_specs, out_specs=out_specs, check_vma=False)
```

```python
import functools

import jax
import jax.numpy as jnp
from jax import lax
from jax.experimental import pallas as pl
from jax.experimental.pallas import tpu as pltpu
from jax.sharding import PartitionSpec as P

MESH = pl.DeviceIdType.MESH
F32 = jnp.float32
BF16 = jnp.bfloat16
LANES = 128


def quotient(number, by):
    if by & (by - 1):
        return number // by
    return lax.shift_right_logical(number, by.bit_length() - 1)


def remainder(number, by):
    return number % by if by & (by - 1) else number & (by - 1)


def kernel(
    n_tm,
    n_rows,
    latent_hbm,
    gain_hbm,
    bias1_hbm,
    bias2_hbm,
    w1_hbm,
    wu_hbm,
    out_ref,
    latent_ref,
    gain_ref,
    bias1_ref,
    bias2_ref,
    w1_ref,
    wpad,
    wu_ref,
    upper,
    send,
    recv,
    shifted,
    part_send,
    part_recv,
    own,
    block,
    pick,
    load_sem,
    act_send_sem,
    act_recv_sem,
    part_send_sem,
    part_recv_sem,
    row_send_sem,
    row_recv_sem,
):
    frames, rows, width, chans = latent_ref.shape
    cells = frames * rows * width
    taps, piece, _ = w1_ref.shape
    outputs = wu_ref.shape[1]
    me = lax.axis_index("tm")
    band = lax.axis_index("rows")
    above = lax.rem(band + n_rows - 1, n_rows)
    below = lax.rem(band + 1, n_rows)
    has_above = band > 0
    has_below = band < n_rows - 1

    load_latent = pltpu.make_async_copy(latent_hbm, latent_ref, load_sem.at[0])
    load_gain = pltpu.make_async_copy(gain_hbm, gain_ref, load_sem.at[1])
    load_w1 = pltpu.make_async_copy(w1_hbm, w1_ref, load_sem.at[2])
    load_bias1 = pltpu.make_async_copy(bias1_hbm, bias1_ref, load_sem.at[3])
    load_wu = pltpu.make_async_copy(wu_hbm, wu_ref, load_sem.at[4])
    load_bias2 = pltpu.make_async_copy(bias2_hbm, bias2_ref, load_sem.at[5])
    for load in (load_latent, load_gain, load_w1, load_bias1, load_wu, load_bias2):
        load.start()

    barrier = pltpu.get_barrier_semaphore()
    for d in range(1, n_tm):
        pl.semaphore_signal(
            barrier, inc=1, device_id=(lax.rem(me + d, n_tm), band), device_id_type=MESH
        )

    @pl.when(has_above)
    def _():
        for s in range(n_tm):
            pl.semaphore_signal(barrier, inc=1, device_id=(s, above), device_id_type=MESH)

    @pl.when(has_below)
    def _():
        for s in range(n_tm):
            pl.semaphore_signal(barrier, inc=1, device_id=(s, below), device_id_type=MESH)

    load_latent.wait()
    load_gain.wait()
    values = latent_ref[...].astype(F32).reshape(cells, chans)
    mean_square = jnp.mean(values * values, axis=-1, keepdims=True)
    scaled = values * lax.rsqrt(mean_square + 1e-06) * gain_ref[...].reshape(1, chans)
    act = scaled / (1.0 + jnp.exp(-scaled))
    blank = jnp.zeros((cells, LANES - piece), F32)
    for s in range(n_tm):
        cut = jnp.concatenate([act[:, s * piece : (s + 1) * piece], blank], axis=1)
        send[s] = cut.astype(BF16).reshape(frames, rows, width, LANES)

    neighbours = jnp.where(has_above, n_tm, 0) + jnp.where(has_below, n_tm, 0)
    pl.semaphore_wait(barrier, n_tm - 1 + neighbours)

    mine = pl.ds(me * frames, frames)

    def act_copy(s, kind, row, where, to):
        return pltpu.make_async_remote_copy(
            src_ref=send.at[s, :, row],
            dst_ref=recv.at[mine, where],
            send_sem=act_send_sem.at[3 * s + kind],
            recv_sem=act_recv_sem.at[3 * me + kind],
            device_id=(s, to),
            device_id_type=MESH,
        )

    def main_copy(s):
        return act_copy(s, 0, pl.ds(0, rows), pl.ds(1, rows), band)

    def down_copy(s):
        return act_copy(s, 1, pl.ds(rows - 1, 1), pl.ds(0, 1), below)

    def up_copy(s):
        return act_copy(s, 2, pl.ds(0, 1), pl.ds(rows + 1, 1), above)

    for d in range(1, n_tm):
        main_copy(lax.rem(me + d, n_tm)).start()

    @pl.when(has_below)
    def _():
        for s in range(n_tm):
            down_copy(s).start()

    @pl.when(has_above)
    def _():
        for s in range(n_tm):
            up_copy(s).start()

    recv[mine, pl.ds(1, rows)] = send[me]
    all_frames = n_tm * frames
    edge = jnp.zeros((all_frames, 1, width, LANES), BF16)
    block_edge = jnp.zeros((frames, 1, width, chans), BF16)

    @pl.when(band == 0)
    def _():
        recv[:, pl.ds(0, 1)] = edge
        block[:, pl.ds(0, 1)] = block_edge

    @pl.when(band == n_rows - 1)
    def _():
        recv[:, pl.ds(rows + 1, 1)] = edge
        block[:, pl.ds(rows + 1, 1)] = block_edge

    shifted[:, pl.ds(0, 2)] = jnp.zeros((3, 2, rows + 2, width, LANES), BF16)

    big = 2 * rows
    depth = block.shape[1]
    block[:, pl.ds(rows + 2, depth - rows - 2)] = jnp.zeros(
        (frames, depth - rows - 2, width, chans), BF16
    )
    at = lax.broadcasted_iota(jnp.int32, (pick.shape[0], 1), 0)
    to = lax.broadcasted_iota(jnp.int32, pick.shape, 1)
    row_tap = quotient(at, frames * width * big)
    col = remainder(quotient(at, frames * big), width)
    frame = remainder(quotient(at, big), frames)
    line = remainder(at, big)
    source = frame * (depth * width) + quotient(line + row_tap + 1, 2) * width + col
    pick[...] = jnp.where(to == source, 1.0, 0.0).astype(BF16)

    load_w1.wait()
    spare = jnp.zeros((LANES - piece, chans), BF16)
    for tap in range(taps):
        wpad[pl.ds(tap * LANES, LANES)] = jnp.concatenate([w1_ref[tap], spare], axis=0)

    def act_arrival(s, kind, row, where):
        return pltpu.make_async_remote_copy(
            src_ref=send.at[s, :, row],
            dst_ref=recv.at[pl.ds(s * frames, frames), where],
            send_sem=act_send_sem.at[3 * s + kind],
            recv_sem=act_recv_sem.at[3 * s + kind],
            device_id=(lax.rem(me + 1, n_tm), band),
            device_id_type=MESH,
        )

    for d in range(1, n_tm):
        s = lax.rem(me + d, n_tm)
        act_arrival(s, 0, pl.ds(0, rows), pl.ds(1, rows)).wait_recv()

    @pl.when(has_above)
    def _():
        for s in range(n_tm):
            act_arrival(s, 1, pl.ds(0, 1), pl.ds(0, 1)).wait_recv()

    @pl.when(has_below)
    def _():
        for s in range(n_tm):
            act_arrival(s, 2, pl.ds(0, 1), pl.ds(rows + 1, 1)).wait_recv()

    tall = all_frames * (rows + 2) * width
    flat = recv[...].astype(F32).reshape(tall, LANES)
    column = remainder(lax.broadcasted_iota(jnp.int32, (tall, LANES), 0), width)
    left = jnp.where(column == 0, 0.0, pltpu.roll(flat, 1, 0))
    right = jnp.where(column == width - 1, 0.0, pltpu.roll(flat, tall - 1, 0))
    shape = (all_frames, rows + 2, width, LANES)
    shifted[0, pl.ds(2, all_frames)] = left.astype(BF16).reshape(shape)
    shifted[1, pl.ds(2, all_frames)] = recv[...]
    shifted[2, pl.ds(2, all_frames)] = right.astype(BF16).reshape(shape)

    pairs = n_tm // 2

    order = [0, rows - 1] + list(range(1, rows - 1))
    spans = (pl.ds(0, 2), pl.ds(2, rows - 2))

    def part_copy(s, kind):
        return pltpu.make_async_remote_copy(
            src_ref=part_send.at[s, :, spans[kind]],
            dst_ref=part_recv.at[me, :, spans[kind]],
            send_sem=part_send_sem.at[2 * s + kind],
            recv_sem=part_recv_sem.at[2 * me + kind],
            device_id=(s, band),
            device_id_type=MESH,
        )

    def part_arrival(s, kind):
        return pltpu.make_async_remote_copy(
            src_ref=part_send.at[s, :, spans[kind]],
            dst_ref=part_recv.at[s, :, spans[kind]],
            send_sem=part_send_sem.at[2 * s + kind],
            recv_sem=part_recv_sem.at[2 * s + kind],
            device_id=(s, band),
            device_id_type=MESH,
        )

    def stage(s, sums):
        for slot, row in enumerate(order):
            part_send[s, :, slot] = sums[:, row].astype(BF16)

    for k in range(1, pairs + 1):
        pair = lax.rem(lax.div(me, 2) + k, pairs)
        total = jnp.zeros((2 * cells, chans), F32)
        for dt in range(3):
            windows = []
            for dy in range(3):
                for dx in range(3):
                    start = pair * (2 * frames) + dt
                    view = shifted[dx, pl.ds(start, 2 * frames), pl.ds(dy, rows)]
                    windows.append(view.reshape(2 * cells, LANES))
            total = total + jnp.dot(
                jnp.concatenate(windows, axis=1),
                wpad[pl.ds(dt * 9 * LANES, 9 * LANES)],
                preferred_element_type=F32,
            )
        sums = total.reshape(2, frames, rows, width, chans)
        if k < pairs:
            for c in range(2):
                stage(2 * pair + c, sums[c])
            for kind in range(2):
                for c in range(2):
                    part_copy(2 * pair + c, kind).start()
        else:
            own[...] = sums
            mate = 2 * lax.div(me, 2) + (1 - lax.rem(me, 2))
            stage(mate, own[1 - lax.rem(me, 2)])
            for kind in range(2):
                part_copy(mate, kind).start()

    load_wu.wait()
    for dx in range(3):
        taken = jnp.concatenate([wu_ref[dx], wu_ref[3 + dx], wu_ref[6 + dx]], axis=1)
        upper[dx] = taken.T

    load_bias1.wait()
    bias1 = bias1_ref[...].reshape(1, 1, chans)

    def finish(kind):
        for d in range(1, n_tm):
            part_arrival(lax.rem(me + n_tm - d, n_tm), kind).wait_recv()
        for slot, row in enumerate(order):
            if (slot >= 2) != (kind == 1):
                continue
            summed = own[lax.rem(me, 2), :, row] + bias1 + latent_ref[:, row].astype(F32)
            for d in range(1, n_tm):
                summed = summed + part_recv[lax.rem(me + n_tm - d, n_tm), :, slot].astype(F32)
            block[:, row + 1] = summed.astype(BF16)

    finish(0)

    def row_copy(kind, row, where, to):
        return pltpu.make_async_remote_copy(
            src_ref=block.at[:, pl.ds(row, 1)],
            dst_ref=block.at[:, pl.ds(where, 1)],
            send_sem=row_send_sem.at[kind],
            recv_sem=row_recv_sem.at[kind],
            device_id=(me, to),
            device_id_type=MESH,
        )

    @pl.when(has_below)
    def _():
        row_copy(0, rows, 0, below).start()

    @pl.when(has_above)
    def _():
        row_copy(1, 1, rows + 1, above).start()

    finish(1)
    load_bias2.wait()

    @pl.when(has_above)
    def _():
        row_copy(0, rows, 0, above).wait_recv()

    @pl.when(has_below)
    def _():
        row_copy(1, 1, rows + 1, below).wait_recv()

    spread = jnp.dot(
        pick[...],
        block[...].reshape(frames * depth * width, chans),
        preferred_element_type=F32,
    ).astype(BF16)
    high = frames * width * big
    lines = jnp.concatenate([spread[k * high : (k + 1) * high] for k in range(3)], axis=1)
    cols = []
    for dx in range(3):
        product = jnp.dot(lines, upper[dx], preferred_element_type=F32)
        cols.append(product.reshape(width, frames * big, outputs))
    nothing = jnp.zeros((1, frames * big, outputs), F32)
    before = jnp.concatenate([nothing, cols[0][: width - 1]], axis=0)
    after = jnp.concatenate([cols[2][1:], nothing], axis=0)
    bias2 = bias2_ref[...].reshape(1, 1, outputs)
    even = before + cols[1] + cols[2] + bias2
    odd = cols[0] + cols[1] + after + bias2
    both = jnp.concatenate([even, odd], axis=-1).astype(BF16)
    for c in range(width):
        out_ref[:, pl.ds(c * 2 * outputs, 2 * outputs)] = both[c]

    for d in range(1, n_tm):
        s = lax.rem(me + d, n_tm)
        main_copy(s).wait_send()
        for kind in range(2):
            part_copy(s, kind).wait_send()

    @pl.when(has_below)
    def _():
        for s in range(n_tm):
            down_copy(s).wait_send()
        row_copy(0, rows, 0, below).wait_send()

    @pl.when(has_above)
    def _():
        for s in range(n_tm):
            up_copy(s).wait_send()
        row_copy(1, 1, rows + 1, above).wait_send()


def local(n_tm, n_rows, latent, gain_first, conv_first, bias_first, conv_upper, bias_upper):
    frames, rows, width, chans = latent.shape
    outputs = conv_upper.shape[2]
    taps, piece, _ = conv_first.shape
    cells = frames * rows * width
    all_frames = n_tm * frames
    depth = rows + 4
    vmem = pl.BlockSpec(memory_space=pltpu.VMEM)
    hbm = pl.BlockSpec(memory_space=pl.ANY)
    dma = pltpu.SemaphoreType.DMA
    flops = 2 * taps * piece * chans * all_frames * rows * width + 18 * 4 * cells * chans * outputs
    decoded = pl.pallas_call(
        functools.partial(kernel, n_tm, n_rows),
        out_shape=jax.ShapeDtypeStruct((frames * 2 * rows, 2 * width * outputs), BF16),
        in_specs=[hbm] * 6,
        out_specs=vmem,
        scratch_shapes=[
            pltpu.VMEM(latent.shape, BF16),
            pltpu.VMEM((chans,), F32),
            pltpu.VMEM((chans,), F32),
            pltpu.VMEM((outputs,), F32),
            pltpu.VMEM(conv_first.shape, BF16),
            pltpu.VMEM((taps * LANES, chans), BF16),
            pltpu.VMEM((9, outputs, chans), BF16),
            pltpu.VMEM((3, 3 * chans, outputs), BF16),
            pltpu.VMEM((n_tm, frames, rows, width, LANES), BF16),
            pltpu.VMEM((all_frames, rows + 2, width, LANES), BF16),
            pltpu.VMEM((3, all_frames + 2, rows + 2, width, LANES), BF16),
            pltpu.VMEM((n_tm, frames, rows, width, chans), BF16),
            pltpu.VMEM((n_tm, frames, rows, width, chans), BF16),
            pltpu.VMEM((2, frames, rows, width, chans), F32),
            pltpu.VMEM((frames, depth, width, chans), BF16),
            pltpu.VMEM((6 * cells, frames * depth * width), BF16),
            dma((6,)),
            dma((3 * n_tm,)),
            dma((3 * n_tm,)),
            dma((2 * n_tm,)),
            dma((2 * n_tm,)),
            dma((2,)),
            dma((2,)),
        ],
        compiler_params=pltpu.CompilerParams(
            collective_id=0, has_side_effects=True, vmem_limit_bytes=60 * 1024 * 1024
        ),
        cost_estimate=pl.CostEstimate(
            flops=flops, bytes_accessed=4 * 1024 * 1024, transcendentals=cells * chans
        ),
    )(
        latent,
        gain_first,
        bias_first,
        bias_upper,
        conv_first,
        jnp.swapaxes(conv_upper, 1, 2),
    )
    return decoded.reshape(frames, 2 * rows, 2 * width * outputs)


def solution(mesh):
    in_specs = (P("tm", "rows", None, None), P(), P(None, "tm", None), P(), P(), P())
    out_specs = P("tm", "rows", None)
    body = functools.partial(local, mesh.shape["tm"], mesh.shape["rows"])
    return jax.shard_map(body, mesh=mesh, in_specs=in_specs, out_specs=out_specs, check_vma=False)
```

```python
import functools

import jax
import jax.numpy as jnp
from jax import lax
from jax.experimental import pallas as pl
from jax.experimental.pallas import tpu as pltpu
from jax.sharding import PartitionSpec as P

MESH = pl.DeviceIdType.MESH
F32 = jnp.float32
BF16 = jnp.bfloat16
LANES = 128


def kernel(
    n_tm,
    n_rows,
    latent_hbm,
    gain_hbm,
    bias1_hbm,
    bias2_hbm,
    w1_hbm,
    wu_hbm,
    out_ref,
    latent_ref,
    gain_ref,
    bias1_ref,
    bias2_ref,
    w1_ref,
    wpad,
    wu_ref,
    send,
    recv,
    shifted,
    part_send,
    part_recv,
    own,
    block,
    pick,
    load_sem,
    act_send_sem,
    act_recv_sem,
    part_send_sem,
    part_recv_sem,
    row_send_sem,
    row_recv_sem,
):
    frames, rows, width, chans = latent_ref.shape
    cells = frames * rows * width
    taps, piece, _ = w1_ref.shape
    outputs = wu_ref.shape[1]
    me = lax.axis_index("tm")
    band = lax.axis_index("rows")
    above = lax.rem(band + n_rows - 1, n_rows)
    below = lax.rem(band + 1, n_rows)
    has_above = band > 0
    has_below = band < n_rows - 1

    load_latent = pltpu.make_async_copy(latent_hbm, latent_ref, load_sem.at[0])
    load_gain = pltpu.make_async_copy(gain_hbm, gain_ref, load_sem.at[1])
    load_w1 = pltpu.make_async_copy(w1_hbm, w1_ref, load_sem.at[2])
    load_bias1 = pltpu.make_async_copy(bias1_hbm, bias1_ref, load_sem.at[3])
    load_wu = pltpu.make_async_copy(wu_hbm, wu_ref, load_sem.at[4])
    load_bias2 = pltpu.make_async_copy(bias2_hbm, bias2_ref, load_sem.at[5])
    for load in (load_latent, load_gain, load_w1, load_bias1, load_wu, load_bias2):
        load.start()

    barrier = pltpu.get_barrier_semaphore()
    for d in range(1, n_tm):
        pl.semaphore_signal(
            barrier, inc=1, device_id=(lax.rem(me + d, n_tm), band), device_id_type=MESH
        )

    @pl.when(has_above)
    def _():
        for s in range(n_tm):
            pl.semaphore_signal(barrier, inc=1, device_id=(s, above), device_id_type=MESH)

    @pl.when(has_below)
    def _():
        for s in range(n_tm):
            pl.semaphore_signal(barrier, inc=1, device_id=(s, below), device_id_type=MESH)

    load_latent.wait()
    load_gain.wait()
    values = latent_ref[...].astype(F32).reshape(cells, chans)
    mean_square = jnp.mean(values * values, axis=-1, keepdims=True)
    scaled = values * lax.rsqrt(mean_square + 1e-06) * gain_ref[...].reshape(1, chans)
    act = scaled / (1.0 + jnp.exp(-scaled))
    blank = jnp.zeros((cells, LANES - piece), F32)
    for s in range(n_tm):
        cut = jnp.concatenate([act[:, s * piece : (s + 1) * piece], blank], axis=1)
        send[s] = cut.astype(BF16).reshape(frames, rows, width, LANES)

    neighbours = jnp.where(has_above, n_tm, 0) + jnp.where(has_below, n_tm, 0)
    pl.semaphore_wait(barrier, n_tm - 1 + neighbours)

    mine = pl.ds(me * frames, frames)

    def act_copy(s, kind, row, where, to):
        return pltpu.make_async_remote_copy(
            src_ref=send.at[s, :, row],
            dst_ref=recv.at[mine, where],
            send_sem=act_send_sem.at[3 * s + kind],
            recv_sem=act_recv_sem.at[3 * me + kind],
            device_id=(s, to),
            device_id_type=MESH,
        )

    def main_copy(s):
        return act_copy(s, 0, pl.ds(0, rows), pl.ds(1, rows), band)

    def down_copy(s):
        return act_copy(s, 1, pl.ds(rows - 1, 1), pl.ds(0, 1), below)

    def up_copy(s):
        return act_copy(s, 2, pl.ds(0, 1), pl.ds(rows + 1, 1), above)

    for d in range(1, n_tm):
        main_copy(lax.rem(me + d, n_tm)).start()

    @pl.when(has_below)
    def _():
        for s in range(n_tm):
            down_copy(s).start()

    @pl.when(has_above)
    def _():
        for s in range(n_tm):
            up_copy(s).start()

    recv[mine, pl.ds(1, rows)] = send[me]
    all_frames = n_tm * frames
    edge = jnp.zeros((all_frames, 1, width, LANES), BF16)
    block_edge = jnp.zeros((frames, 1, width, chans), BF16)

    @pl.when(band == 0)
    def _():
        recv[:, pl.ds(0, 1)] = edge
        block[:, pl.ds(0, 1)] = block_edge

    @pl.when(band == n_rows - 1)
    def _():
        recv[:, pl.ds(rows + 1, 1)] = edge
        block[:, pl.ds(rows + 1, 1)] = block_edge

    shifted[:, pl.ds(0, 2)] = jnp.zeros((3, 2, rows + 2, width, LANES), BF16)

    big = 2 * rows
    depth = block.shape[1]
    block[:, pl.ds(rows + 2, depth - rows - 2)] = jnp.zeros(
        (frames, depth - rows - 2, width, chans), BF16
    )
    at = lax.broadcasted_iota(jnp.int32, (pick.shape[0], 1), 0)
    to = lax.broadcasted_iota(jnp.int32, pick.shape, 1)
    row_tap = at // (frames * width * big)
    col = (at // (frames * big)) % width
    frame = (at // big) % frames
    line = at % big
    source = frame * (depth * width) + ((line + row_tap + 1) // 2) * width + col
    pick[...] = jnp.where(to == source, 1.0, 0.0).astype(BF16)

    load_w1.wait()
    spare = jnp.zeros((LANES - piece, chans), BF16)
    for tap in range(taps):
        wpad[pl.ds(tap * LANES, LANES)] = jnp.concatenate([w1_ref[tap], spare], axis=0)

    def act_arrival(s, kind, row, where):
        return pltpu.make_async_remote_copy(
            src_ref=send.at[s, :, row],
            dst_ref=recv.at[pl.ds(s * frames, frames), where],
            send_sem=act_send_sem.at[3 * s + kind],
            recv_sem=act_recv_sem.at[3 * s + kind],
            device_id=(lax.rem(me + 1, n_tm), band),
            device_id_type=MESH,
        )

    for d in range(1, n_tm):
        s = lax.rem(me + d, n_tm)
        act_arrival(s, 0, pl.ds(0, rows), pl.ds(1, rows)).wait_recv()

    @pl.when(has_above)
    def _():
        for s in range(n_tm):
            act_arrival(s, 1, pl.ds(0, 1), pl.ds(0, 1)).wait_recv()

    @pl.when(has_below)
    def _():
        for s in range(n_tm):
            act_arrival(s, 2, pl.ds(0, 1), pl.ds(rows + 1, 1)).wait_recv()

    tall = all_frames * (rows + 2) * width
    flat = recv[...].astype(F32).reshape(tall, LANES)
    column = lax.broadcasted_iota(jnp.int32, (tall, LANES), 0) % width
    left = jnp.where(column == 0, 0.0, pltpu.roll(flat, 1, 0))
    right = jnp.where(column == width - 1, 0.0, pltpu.roll(flat, tall - 1, 0))
    shape = (all_frames, rows + 2, width, LANES)
    shifted[0, pl.ds(2, all_frames)] = left.astype(BF16).reshape(shape)
    shifted[1, pl.ds(2, all_frames)] = recv[...]
    shifted[2, pl.ds(2, all_frames)] = right.astype(BF16).reshape(shape)

    pairs = n_tm // 2

    order = [0, rows - 1] + list(range(1, rows - 1))
    spans = (pl.ds(0, 2), pl.ds(2, rows - 2))

    def part_copy(s, kind):
        return pltpu.make_async_remote_copy(
            src_ref=part_send.at[s, :, spans[kind]],
            dst_ref=part_recv.at[me, :, spans[kind]],
            send_sem=part_send_sem.at[2 * s + kind],
            recv_sem=part_recv_sem.at[2 * me + kind],
            device_id=(s, band),
            device_id_type=MESH,
        )

    def part_arrival(s, kind):
        return pltpu.make_async_remote_copy(
            src_ref=part_send.at[s, :, spans[kind]],
            dst_ref=part_recv.at[s, :, spans[kind]],
            send_sem=part_send_sem.at[2 * s + kind],
            recv_sem=part_recv_sem.at[2 * s + kind],
            device_id=(s, band),
            device_id_type=MESH,
        )

    def stage(s, sums):
        for slot, row in enumerate(order):
            part_send[s, :, slot] = sums[:, row].astype(BF16)

    for k in range(1, pairs + 1):
        pair = lax.rem(lax.div(me, 2) + k, pairs)
        windows = []
        for dt in range(3):
            for dy in range(3):
                for dx in range(3):
                    start = pair * (2 * frames) + dt
                    view = shifted[dx, pl.ds(start, 2 * frames), pl.ds(dy, rows)]
                    windows.append(view.reshape(2 * cells, LANES))
        total = jnp.dot(
            jnp.concatenate(windows, axis=1), wpad[...], preferred_element_type=F32
        )
        sums = total.reshape(2, frames, rows, width, chans)
        if k < pairs:
            for c in range(2):
                stage(2 * pair + c, sums[c])
            for kind in range(2):
                for c in range(2):
                    part_copy(2 * pair + c, kind).start()
        else:
            own[...] = sums
            mate = 2 * lax.div(me, 2) + (1 - lax.rem(me, 2))
            stage(mate, own[1 - lax.rem(me, 2)])
            for kind in range(2):
                part_copy(mate, kind).start()

    load_bias1.wait()
    bias1 = bias1_ref[...].reshape(1, 1, chans)

    def finish(kind):
        for d in range(1, n_tm):
            part_arrival(lax.rem(me + n_tm - d, n_tm), kind).wait_recv()
        for slot, row in enumerate(order):
            if (slot >= 2) != (kind == 1):
                continue
            summed = own[lax.rem(me, 2), :, row] + bias1 + latent_ref[:, row].astype(F32)
            for d in range(1, n_tm):
                summed = summed + part_recv[lax.rem(me + n_tm - d, n_tm), :, slot].astype(F32)
            block[:, row + 1] = summed.astype(BF16)

    finish(0)

    def row_copy(kind, row, where, to):
        return pltpu.make_async_remote_copy(
            src_ref=block.at[:, pl.ds(row, 1)],
            dst_ref=block.at[:, pl.ds(where, 1)],
            send_sem=row_send_sem.at[kind],
            recv_sem=row_recv_sem.at[kind],
            device_id=(me, to),
            device_id_type=MESH,
        )

    @pl.when(has_below)
    def _():
        row_copy(0, rows, 0, below).start()

    @pl.when(has_above)
    def _():
        row_copy(1, 1, rows + 1, above).start()

    finish(1)
    load_wu.wait()
    load_bias2.wait()

    @pl.when(has_above)
    def _():
        row_copy(0, rows, 0, above).wait_recv()

    @pl.when(has_below)
    def _():
        row_copy(1, 1, rows + 1, below).wait_recv()

    spread = jnp.dot(
        pick[...],
        block[...].reshape(frames * depth * width, chans),
        preferred_element_type=F32,
    ).astype(BF16)
    high = frames * width * big
    lines = jnp.concatenate([spread[k * high : (k + 1) * high] for k in range(3)], axis=1)
    cols = []
    for dx in range(3):
        weights = jnp.concatenate([wu_ref[dx], wu_ref[3 + dx], wu_ref[6 + dx]], axis=1)
        product = lax.dot_general(
            lines, weights, (((1,), (1,)), ((), ())), preferred_element_type=F32
        )
        cols.append(product.reshape(width, frames * big, outputs))
    nothing = jnp.zeros((1, frames * big, outputs), F32)
    before = jnp.concatenate([nothing, cols[0][: width - 1]], axis=0)
    after = jnp.concatenate([cols[2][1:], nothing], axis=0)
    bias2 = bias2_ref[...].reshape(1, 1, outputs)
    even = before + cols[1] + cols[2] + bias2
    odd = cols[0] + cols[1] + after + bias2
    both = jnp.concatenate([even, odd], axis=-1).astype(BF16)
    for c in range(width):
        out_ref[:, pl.ds(c * 2 * outputs, 2 * outputs)] = both[c]

    for d in range(1, n_tm):
        s = lax.rem(me + d, n_tm)
        main_copy(s).wait_send()
        for kind in range(2):
            part_copy(s, kind).wait_send()

    @pl.when(has_below)
    def _():
        for s in range(n_tm):
            down_copy(s).wait_send()
        row_copy(0, rows, 0, below).wait_send()

    @pl.when(has_above)
    def _():
        for s in range(n_tm):
            up_copy(s).wait_send()
        row_copy(1, 1, rows + 1, above).wait_send()


def local(n_tm, n_rows, latent, gain_first, conv_first, bias_first, conv_upper, bias_upper):
    frames, rows, width, chans = latent.shape
    outputs = conv_upper.shape[2]
    taps, piece, _ = conv_first.shape
    cells = frames * rows * width
    all_frames = n_tm * frames
    depth = rows + 4
    vmem = pl.BlockSpec(memory_space=pltpu.VMEM)
    hbm = pl.BlockSpec(memory_space=pl.ANY)
    dma = pltpu.SemaphoreType.DMA
    flops = 2 * taps * piece * chans * all_frames * rows * width + 18 * 4 * cells * chans * outputs
    decoded = pl.pallas_call(
        functools.partial(kernel, n_tm, n_rows),
        out_shape=jax.ShapeDtypeStruct((frames * 2 * rows, 2 * width * outputs), BF16),
        in_specs=[hbm] * 6,
        out_specs=vmem,
        scratch_shapes=[
            pltpu.VMEM(latent.shape, BF16),
            pltpu.VMEM((chans,), F32),
            pltpu.VMEM((chans,), F32),
            pltpu.VMEM((outputs,), F32),
            pltpu.VMEM(conv_first.shape, BF16),
            pltpu.VMEM((taps * LANES, chans), BF16),
            pltpu.VMEM((9, outputs, chans), BF16),
            pltpu.VMEM((n_tm, frames, rows, width, LANES), BF16),
            pltpu.VMEM((all_frames, rows + 2, width, LANES), BF16),
            pltpu.VMEM((3, all_frames + 2, rows + 2, width, LANES), BF16),
            pltpu.VMEM((n_tm, frames, rows, width, chans), BF16),
            pltpu.VMEM((n_tm, frames, rows, width, chans), BF16),
            pltpu.VMEM((2, frames, rows, width, chans), F32),
            pltpu.VMEM((frames, depth, width, chans), BF16),
            pltpu.VMEM((6 * cells, frames * depth * width), BF16),
            dma((6,)),
            dma((3 * n_tm,)),
            dma((3 * n_tm,)),
            dma((2 * n_tm,)),
            dma((2 * n_tm,)),
            dma((2,)),
            dma((2,)),
        ],
        compiler_params=pltpu.CompilerParams(
            collective_id=0, has_side_effects=True, vmem_limit_bytes=60 * 1024 * 1024
        ),
        cost_estimate=pl.CostEstimate(
            flops=flops, bytes_accessed=4 * 1024 * 1024, transcendentals=cells * chans
        ),
    )(
        latent,
        gain_first,
        bias_first,
        bias_upper,
        conv_first,
        jnp.swapaxes(conv_upper, 1, 2),
    )
    return decoded.reshape(frames, 2 * rows, 2 * width * outputs)


def solution(mesh):
    in_specs = (P("tm", "rows", None, None), P(), P(None, "tm", None), P(), P(), P())
    out_specs = P("tm", "rows", None)
    body = functools.partial(local, mesh.shape["tm"], mesh.shape["rows"])
    return jax.shard_map(body, mesh=mesh, in_specs=in_specs, out_specs=out_specs, check_vma=False)
```

```python
import functools

import jax
import jax.numpy as jnp
from jax import lax
from jax.experimental import pallas as pl
from jax.experimental.pallas import tpu as pltpu
from jax.sharding import PartitionSpec as P

MESH = pl.DeviceIdType.MESH
F32 = jnp.float32
BF16 = jnp.bfloat16
LANES = 128


def kernel(
    n_tm,
    n_rows,
    latent_hbm,
    gain_hbm,
    bias1_hbm,
    bias2_hbm,
    w1_hbm,
    wu_hbm,
    out_ref,
    latent_ref,
    gain_ref,
    bias1_ref,
    bias2_ref,
    w1_ref,
    wpad,
    wu_ref,
    send,
    recv,
    shifted,
    part_send,
    part_recv,
    own,
    block,
    pick,
    load_sem,
    act_send_sem,
    act_recv_sem,
    part_send_sem,
    part_recv_sem,
    row_send_sem,
    row_recv_sem,
):
    frames, rows, width, chans = latent_ref.shape
    cells = frames * rows * width
    taps, piece, _ = w1_ref.shape
    outputs = wu_ref.shape[1]
    me = lax.axis_index("tm")
    band = lax.axis_index("rows")
    above = lax.rem(band + n_rows - 1, n_rows)
    below = lax.rem(band + 1, n_rows)
    has_above = band > 0
    has_below = band < n_rows - 1

    load_latent = pltpu.make_async_copy(latent_hbm, latent_ref, load_sem.at[0])
    load_gain = pltpu.make_async_copy(gain_hbm, gain_ref, load_sem.at[1])
    load_w1 = pltpu.make_async_copy(w1_hbm, w1_ref, load_sem.at[2])
    load_bias1 = pltpu.make_async_copy(bias1_hbm, bias1_ref, load_sem.at[3])
    load_wu = pltpu.make_async_copy(wu_hbm, wu_ref, load_sem.at[4])
    load_bias2 = pltpu.make_async_copy(bias2_hbm, bias2_ref, load_sem.at[5])
    for load in (load_latent, load_gain, load_w1, load_bias1, load_wu, load_bias2):
        load.start()

    barrier = pltpu.get_barrier_semaphore()
    for d in range(1, n_tm):
        pl.semaphore_signal(
            barrier, inc=1, device_id=(lax.rem(me + d, n_tm), band), device_id_type=MESH
        )

    @pl.when(has_above)
    def _():
        for s in range(n_tm):
            pl.semaphore_signal(barrier, inc=1, device_id=(s, above), device_id_type=MESH)

    @pl.when(has_below)
    def _():
        for s in range(n_tm):
            pl.semaphore_signal(barrier, inc=1, device_id=(s, below), device_id_type=MESH)

    load_latent.wait()
    load_gain.wait()
    values = latent_ref[...].astype(F32).reshape(cells, chans)
    mean_square = jnp.mean(values * values, axis=-1, keepdims=True)
    scaled = values * lax.rsqrt(mean_square + 1e-06) * gain_ref[...].reshape(1, chans)
    act = scaled / (1.0 + jnp.exp(-scaled))
    blank = jnp.zeros((cells, LANES - piece), F32)
    for s in range(n_tm):
        cut = jnp.concatenate([act[:, s * piece : (s + 1) * piece], blank], axis=1)
        send[s] = cut.astype(BF16).reshape(frames, rows, width, LANES)

    neighbours = jnp.where(has_above, n_tm, 0) + jnp.where(has_below, n_tm, 0)
    pl.semaphore_wait(barrier, n_tm - 1 + neighbours)

    mine = pl.ds(me * frames, frames)

    def act_copy(s, kind, row, where, to):
        return pltpu.make_async_remote_copy(
            src_ref=send.at[s, :, row],
            dst_ref=recv.at[mine, where],
            send_sem=act_send_sem.at[3 * s + kind],
            recv_sem=act_recv_sem.at[3 * me + kind],
            device_id=(s, to),
            device_id_type=MESH,
        )

    def main_copy(s):
        return act_copy(s, 0, pl.ds(0, rows), pl.ds(1, rows), band)

    def down_copy(s):
        return act_copy(s, 1, pl.ds(rows - 1, 1), pl.ds(0, 1), below)

    def up_copy(s):
        return act_copy(s, 2, pl.ds(0, 1), pl.ds(rows + 1, 1), above)

    for d in range(1, n_tm):
        main_copy(lax.rem(me + d, n_tm)).start()

    @pl.when(has_below)
    def _():
        for s in range(n_tm):
            down_copy(s).start()

    @pl.when(has_above)
    def _():
        for s in range(n_tm):
            up_copy(s).start()

    recv[mine, pl.ds(1, rows)] = send[me]
    all_frames = n_tm * frames
    edge = jnp.zeros((all_frames, 1, width, LANES), BF16)
    block_edge = jnp.zeros((frames, 1, width, chans), BF16)

    @pl.when(band == 0)
    def _():
        recv[:, pl.ds(0, 1)] = edge
        block[:, pl.ds(0, 1)] = block_edge

    @pl.when(band == n_rows - 1)
    def _():
        recv[:, pl.ds(rows + 1, 1)] = edge
        block[:, pl.ds(rows + 1, 1)] = block_edge

    shifted[:, pl.ds(0, 2)] = jnp.zeros((3, 2, rows + 2, width, LANES), BF16)

    big = 2 * rows
    depth = block.shape[1]
    block[:, pl.ds(rows + 2, depth - rows - 2)] = jnp.zeros(
        (frames, depth - rows - 2, width, chans), BF16
    )
    at = lax.broadcasted_iota(jnp.int32, (pick.shape[0], 1), 0)
    to = lax.broadcasted_iota(jnp.int32, pick.shape, 1)
    row_tap = at // (frames * width * big)
    col = (at // (frames * big)) % width
    frame = (at // big) % frames
    line = at % big
    source = frame * (depth * width) + ((line + row_tap + 1) // 2) * width + col
    pick[...] = jnp.where(to == source, 1.0, 0.0).astype(BF16)

    load_w1.wait()
    spare = jnp.zeros((LANES - piece, chans), BF16)
    for tap in range(taps):
        wpad[pl.ds(tap * LANES, LANES)] = jnp.concatenate([w1_ref[tap], spare], axis=0)

    def act_arrival(s, kind, row, where):
        return pltpu.make_async_remote_copy(
            src_ref=send.at[s, :, row],
            dst_ref=recv.at[pl.ds(s * frames, frames), where],
            send_sem=act_send_sem.at[3 * s + kind],
            recv_sem=act_recv_sem.at[3 * s + kind],
            device_id=(lax.rem(me + 1, n_tm), band),
            device_id_type=MESH,
        )

    for d in range(1, n_tm):
        s = lax.rem(me + d, n_tm)
        act_arrival(s, 0, pl.ds(0, rows), pl.ds(1, rows)).wait_recv()

    @pl.when(has_above)
    def _():
        for s in range(n_tm):
            act_arrival(s, 1, pl.ds(0, 1), pl.ds(0, 1)).wait_recv()

    @pl.when(has_below)
    def _():
        for s in range(n_tm):
            act_arrival(s, 2, pl.ds(0, 1), pl.ds(rows + 1, 1)).wait_recv()

    tall = all_frames * (rows + 2) * width
    flat = recv[...].astype(F32).reshape(tall, LANES)
    column = lax.broadcasted_iota(jnp.int32, (tall, LANES), 0) % width
    left = jnp.where(column == 0, 0.0, pltpu.roll(flat, 1, 0))
    right = jnp.where(column == width - 1, 0.0, pltpu.roll(flat, tall - 1, 0))
    shape = (all_frames, rows + 2, width, LANES)
    shifted[0, pl.ds(2, all_frames)] = left.astype(BF16).reshape(shape)
    shifted[1, pl.ds(2, all_frames)] = recv[...]
    shifted[2, pl.ds(2, all_frames)] = right.astype(BF16).reshape(shape)

    pairs = n_tm // 2

    order = [0, rows - 1] + list(range(1, rows - 1))
    spans = (pl.ds(0, 2), pl.ds(2, rows - 2))

    def part_copy(s, kind):
        return pltpu.make_async_remote_copy(
            src_ref=part_send.at[s, :, spans[kind]],
            dst_ref=part_recv.at[me, :, spans[kind]],
            send_sem=part_send_sem.at[2 * s + kind],
            recv_sem=part_recv_sem.at[2 * me + kind],
            device_id=(s, band),
            device_id_type=MESH,
        )

    def part_arrival(s, kind):
        return pltpu.make_async_remote_copy(
            src_ref=part_send.at[s, :, spans[kind]],
            dst_ref=part_recv.at[s, :, spans[kind]],
            send_sem=part_send_sem.at[2 * s + kind],
            recv_sem=part_recv_sem.at[2 * s + kind],
            device_id=(s, band),
            device_id_type=MESH,
        )

    def stage(s, sums):
        for slot, row in enumerate(order):
            part_send[s, :, slot] = sums[:, row].astype(BF16)

    for k in range(1, pairs + 1):
        pair = lax.rem(lax.div(me, 2) + k, pairs)
        total = jnp.zeros((2 * cells, chans), F32)
        for dt in range(3):
            windows = []
            for dy in range(3):
                for dx in range(3):
                    start = pair * (2 * frames) + dt
                    view = shifted[dx, pl.ds(start, 2 * frames), pl.ds(dy, rows)]
                    windows.append(view.reshape(2 * cells, LANES))
            total = total + jnp.dot(
                jnp.concatenate(windows, axis=1),
                wpad[pl.ds(dt * 9 * LANES, 9 * LANES)],
                preferred_element_type=F32,
            )
        sums = total.reshape(2, frames, rows, width, chans)
        if k < pairs:
            for c in range(2):
                stage(2 * pair + c, sums[c])
            for kind in range(2):
                for c in range(2):
                    part_copy(2 * pair + c, kind).start()
        else:
            own[...] = sums
            mate = 2 * lax.div(me, 2) + (1 - lax.rem(me, 2))
            stage(mate, own[1 - lax.rem(me, 2)])
            for kind in range(2):
                part_copy(mate, kind).start()

    load_bias1.wait()
    bias1 = bias1_ref[...].reshape(1, 1, chans)

    def finish(kind):
        for d in range(1, n_tm):
            part_arrival(lax.rem(me + n_tm - d, n_tm), kind).wait_recv()
        for slot, row in enumerate(order):
            if (slot >= 2) != (kind == 1):
                continue
            summed = own[lax.rem(me, 2), :, row] + bias1 + latent_ref[:, row].astype(F32)
            for d in range(1, n_tm):
                summed = summed + part_recv[lax.rem(me + n_tm - d, n_tm), :, slot].astype(F32)
            block[:, row + 1] = summed.astype(BF16)

    finish(0)

    def row_copy(kind, row, where, to):
        return pltpu.make_async_remote_copy(
            src_ref=block.at[:, pl.ds(row, 1)],
            dst_ref=block.at[:, pl.ds(where, 1)],
            send_sem=row_send_sem.at[kind],
            recv_sem=row_recv_sem.at[kind],
            device_id=(me, to),
            device_id_type=MESH,
        )

    @pl.when(has_below)
    def _():
        row_copy(0, rows, 0, below).start()

    @pl.when(has_above)
    def _():
        row_copy(1, 1, rows + 1, above).start()

    finish(1)
    load_wu.wait()
    load_bias2.wait()

    @pl.when(has_above)
    def _():
        row_copy(0, rows, 0, above).wait_recv()

    @pl.when(has_below)
    def _():
        row_copy(1, 1, rows + 1, below).wait_recv()

    spread = jnp.dot(
        pick[...],
        block[...].reshape(frames * depth * width, chans),
        preferred_element_type=F32,
    ).astype(BF16)
    high = frames * width * big
    lines = jnp.concatenate([spread[k * high : (k + 1) * high] for k in range(3)], axis=1)
    cols = []
    for dx in range(3):
        weights = jnp.concatenate([wu_ref[dx], wu_ref[3 + dx], wu_ref[6 + dx]], axis=1)
        product = lax.dot_general(
            lines, weights, (((1,), (1,)), ((), ())), preferred_element_type=F32
        )
        cols.append(product.reshape(width, frames * big, outputs))
    nothing = jnp.zeros((1, frames * big, outputs), F32)
    before = jnp.concatenate([nothing, cols[0][: width - 1]], axis=0)
    after = jnp.concatenate([cols[2][1:], nothing], axis=0)
    bias2 = bias2_ref[...].reshape(1, 1, outputs)
    even = before + cols[1] + cols[2] + bias2
    odd = cols[0] + cols[1] + after + bias2
    both = jnp.concatenate([even, odd], axis=-1).astype(BF16)
    for c in range(width):
        out_ref[:, pl.ds(c * 2 * outputs, 2 * outputs)] = both[c]

    for d in range(1, n_tm):
        s = lax.rem(me + d, n_tm)
        main_copy(s).wait_send()
        for kind in range(2):
            part_copy(s, kind).wait_send()

    @pl.when(has_below)
    def _():
        for s in range(n_tm):
            down_copy(s).wait_send()
        row_copy(0, rows, 0, below).wait_send()

    @pl.when(has_above)
    def _():
        for s in range(n_tm):
            up_copy(s).wait_send()
        row_copy(1, 1, rows + 1, above).wait_send()


def deliver(held_hbm, out_hbm, sems):
    count = sems.shape[0]
    width = out_hbm.shape[1] // count
    copies = []
    for k in range(count):
        part = pl.ds(k * width, width)
        copies.append(pltpu.make_async_copy(held_hbm.at[:, part], out_hbm.at[:, part], sems.at[k]))
    for copy in copies:
        copy.start()
    for copy in copies:
        copy.wait()


def local(n_tm, n_rows, latent, gain_first, conv_first, bias_first, conv_upper, bias_upper):
    frames, rows, width, chans = latent.shape
    outputs = conv_upper.shape[2]
    taps, piece, _ = conv_first.shape
    cells = frames * rows * width
    all_frames = n_tm * frames
    depth = rows + 4
    vmem = pl.BlockSpec(memory_space=pltpu.VMEM)
    hbm = pl.BlockSpec(memory_space=pl.ANY)
    dma = pltpu.SemaphoreType.DMA
    flops = 2 * taps * piece * chans * all_frames * rows * width + 18 * 4 * cells * chans * outputs
    decoded = pl.pallas_call(
        functools.partial(kernel, n_tm, n_rows),
        out_shape=jax.ShapeDtypeStruct((frames * 2 * rows, 2 * width * outputs), BF16),
        in_specs=[hbm] * 6,
        out_specs=vmem,
        scratch_shapes=[
            pltpu.VMEM(latent.shape, BF16),
            pltpu.VMEM((chans,), F32),
            pltpu.VMEM((chans,), F32),
            pltpu.VMEM((outputs,), F32),
            pltpu.VMEM(conv_first.shape, BF16),
            pltpu.VMEM((taps * LANES, chans), BF16),
            pltpu.VMEM((9, outputs, chans), BF16),
            pltpu.VMEM((n_tm, frames, rows, width, LANES), BF16),
            pltpu.VMEM((all_frames, rows + 2, width, LANES), BF16),
            pltpu.VMEM((3, all_frames + 2, rows + 2, width, LANES), BF16),
            pltpu.VMEM((n_tm, frames, rows, width, chans), BF16),
            pltpu.VMEM((n_tm, frames, rows, width, chans), BF16),
            pltpu.VMEM((2, frames, rows, width, chans), F32),
            pltpu.VMEM((frames, depth, width, chans), BF16),
            pltpu.VMEM((6 * cells, frames * depth * width), BF16),
            dma((6,)),
            dma((3 * n_tm,)),
            dma((3 * n_tm,)),
            dma((2 * n_tm,)),
            dma((2 * n_tm,)),
            dma((2,)),
            dma((2,)),
        ],
        compiler_params=pltpu.CompilerParams(
            collective_id=0, has_side_effects=True, vmem_limit_bytes=60 * 1024 * 1024
        ),
        cost_estimate=pl.CostEstimate(
            flops=flops, bytes_accessed=4 * 1024 * 1024, transcendentals=cells * chans
        ),
    )(
        latent,
        gain_first,
        bias_first,
        bias_upper,
        conv_first,
        jnp.swapaxes(conv_upper, 1, 2),
    )
    decoded = pl.pallas_call(
        deliver,
        out_shape=jax.ShapeDtypeStruct(decoded.shape, BF16),
        in_specs=[hbm],
        out_specs=hbm,
        scratch_shapes=[dma((4,))],
    )(decoded)
    return decoded.reshape(frames, 2 * rows, 2 * width * outputs)


def solution(mesh):
    in_specs = (P("tm", "rows", None, None), P(), P(None, "tm", None), P(), P(), P())
    out_specs = P("tm", "rows", None)
    body = functools.partial(local, mesh.shape["tm"], mesh.shape["rows"])
    return jax.shard_map(body, mesh=mesh, in_specs=in_specs, out_specs=out_specs, check_vma=False)
```

```python
import functools

import jax
import jax.numpy as jnp
from jax import lax
from jax.experimental import pallas as pl
from jax.experimental.pallas import tpu as pltpu
from jax.sharding import PartitionSpec as P

MESH = pl.DeviceIdType.MESH
F32 = jnp.float32
BF16 = jnp.bfloat16
LANES = 128


def kernel(
    n_tm,
    n_rows,
    latent_hbm,
    gain_hbm,
    bias1_hbm,
    bias2_hbm,
    w1_hbm,
    wu_hbm,
    out_ref,
    latent_ref,
    gain_ref,
    bias1_ref,
    bias2_ref,
    w1_ref,
    wpad,
    wu_ref,
    send,
    recv,
    shifted,
    part_send,
    part_recv,
    own,
    block,
    pick,
    load_sem,
    act_send_sem,
    act_recv_sem,
    part_send_sem,
    part_recv_sem,
    row_send_sem,
    row_recv_sem,
):
    frames, rows, width, chans = latent_ref.shape
    cells = frames * rows * width
    taps, piece, _ = w1_ref.shape
    outputs = wu_ref.shape[1]
    me = lax.axis_index("tm")
    band = lax.axis_index("rows")
    above = lax.rem(band + n_rows - 1, n_rows)
    below = lax.rem(band + 1, n_rows)
    has_above = band > 0
    has_below = band < n_rows - 1

    load_latent = pltpu.make_async_copy(latent_hbm, latent_ref, load_sem.at[0])
    load_gain = pltpu.make_async_copy(gain_hbm, gain_ref, load_sem.at[1])
    load_w1 = pltpu.make_async_copy(w1_hbm, w1_ref, load_sem.at[2])
    load_bias1 = pltpu.make_async_copy(bias1_hbm, bias1_ref, load_sem.at[3])
    load_wu = pltpu.make_async_copy(wu_hbm, wu_ref, load_sem.at[4])
    load_bias2 = pltpu.make_async_copy(bias2_hbm, bias2_ref, load_sem.at[5])
    for load in (load_latent, load_gain, load_w1, load_bias1, load_wu, load_bias2):
        load.start()

    barrier = pltpu.get_barrier_semaphore()
    for d in range(1, n_tm):
        pl.semaphore_signal(
            barrier, inc=1, device_id=(lax.rem(me + d, n_tm), band), device_id_type=MESH
        )

    @pl.when(has_above)
    def _():
        for s in range(n_tm):
            pl.semaphore_signal(barrier, inc=1, device_id=(s, above), device_id_type=MESH)

    @pl.when(has_below)
    def _():
        for s in range(n_tm):
            pl.semaphore_signal(barrier, inc=1, device_id=(s, below), device_id_type=MESH)

    load_latent.wait()
    load_gain.wait()
    values = latent_ref[...].astype(F32).reshape(cells, chans)
    mean_square = jnp.mean(values * values, axis=-1, keepdims=True)
    scaled = values * lax.rsqrt(mean_square + 1e-06) * gain_ref[...].reshape(1, chans)
    act = scaled / (1.0 + jnp.exp(-scaled))
    blank = jnp.zeros((cells, LANES - piece), F32)
    for s in range(n_tm):
        cut = jnp.concatenate([act[:, s * piece : (s + 1) * piece], blank], axis=1)
        send[s] = cut.astype(BF16).reshape(frames, rows, width, LANES)

    neighbours = jnp.where(has_above, n_tm, 0) + jnp.where(has_below, n_tm, 0)
    pl.semaphore_wait(barrier, n_tm - 1 + neighbours)

    mine = pl.ds(me * frames, frames)

    def act_copy(s, kind, row, where, to):
        return pltpu.make_async_remote_copy(
            src_ref=send.at[s, :, row],
            dst_ref=recv.at[mine, where],
            send_sem=act_send_sem.at[3 * s + kind],
            recv_sem=act_recv_sem.at[3 * me + kind],
            device_id=(s, to),
            device_id_type=MESH,
        )

    def main_copy(s):
        return act_copy(s, 0, pl.ds(0, rows), pl.ds(1, rows), band)

    def down_copy(s):
        return act_copy(s, 1, pl.ds(rows - 1, 1), pl.ds(0, 1), below)

    def up_copy(s):
        return act_copy(s, 2, pl.ds(0, 1), pl.ds(rows + 1, 1), above)

    @pl.when(has_below)
    def _():
        for s in range(n_tm):
            down_copy(s).start()

    @pl.when(has_above)
    def _():
        for s in range(n_tm):
            up_copy(s).start()

    for d in range(1, n_tm):
        main_copy(lax.rem(me + d, n_tm)).start()

    recv[mine, pl.ds(1, rows)] = send[me]
    all_frames = n_tm * frames
    edge = jnp.zeros((all_frames, 1, width, LANES), BF16)
    block_edge = jnp.zeros((frames, 1, width, chans), BF16)

    @pl.when(band == 0)
    def _():
        recv[:, pl.ds(0, 1)] = edge
        block[:, pl.ds(0, 1)] = block_edge

    @pl.when(band == n_rows - 1)
    def _():
        recv[:, pl.ds(rows + 1, 1)] = edge
        block[:, pl.ds(rows + 1, 1)] = block_edge

    shifted[:, pl.ds(0, 2)] = jnp.zeros((3, 2, rows + 2, width, LANES), BF16)

    big = 2 * rows
    depth = block.shape[1]
    block[:, pl.ds(rows + 2, depth - rows - 2)] = jnp.zeros(
        (frames, depth - rows - 2, width, chans), BF16
    )
    at = lax.broadcasted_iota(jnp.int32, (pick.shape[0], 1), 0)
    to = lax.broadcasted_iota(jnp.int32, pick.shape, 1)
    row_tap = at // (frames * width * big)
    col = (at // (frames * big)) % width
    frame = (at // big) % frames
    line = at % big
    source = frame * (depth * width) + ((line + row_tap + 1) // 2) * width + col
    pick[...] = jnp.where(to == source, 1.0, 0.0).astype(BF16)

    load_w1.wait()
    spare = jnp.zeros((LANES - piece, chans), BF16)
    for tap in range(taps):
        wpad[pl.ds(tap * LANES, LANES)] = jnp.concatenate([w1_ref[tap], spare], axis=0)

    def act_arrival(s, kind, row, where):
        return pltpu.make_async_remote_copy(
            src_ref=send.at[s, :, row],
            dst_ref=recv.at[pl.ds(s * frames, frames), where],
            send_sem=act_send_sem.at[3 * s + kind],
            recv_sem=act_recv_sem.at[3 * s + kind],
            device_id=(lax.rem(me + 1, n_tm), band),
            device_id_type=MESH,
        )

    for d in range(1, n_tm):
        s = lax.rem(me + d, n_tm)
        act_arrival(s, 0, pl.ds(0, rows), pl.ds(1, rows)).wait_recv()

    @pl.when(has_above)
    def _():
        for s in range(n_tm):
            act_arrival(s, 1, pl.ds(0, 1), pl.ds(0, 1)).wait_recv()

    @pl.when(has_below)
    def _():
        for s in range(n_tm):
            act_arrival(s, 2, pl.ds(0, 1), pl.ds(rows + 1, 1)).wait_recv()

    tall = all_frames * (rows + 2) * width
    flat = recv[...].astype(F32).reshape(tall, LANES)
    column = lax.broadcasted_iota(jnp.int32, (tall, LANES), 0) % width
    left = jnp.where(column == 0, 0.0, pltpu.roll(flat, 1, 0))
    right = jnp.where(column == width - 1, 0.0, pltpu.roll(flat, tall - 1, 0))
    shape = (all_frames, rows + 2, width, LANES)
    shifted[0, pl.ds(2, all_frames)] = left.astype(BF16).reshape(shape)
    shifted[1, pl.ds(2, all_frames)] = recv[...]
    shifted[2, pl.ds(2, all_frames)] = right.astype(BF16).reshape(shape)

    pairs = n_tm // 2

    order = [0, rows - 1] + list(range(1, rows - 1))
    spans = (pl.ds(0, 2), pl.ds(2, rows - 2))

    def part_copy(s, kind):
        return pltpu.make_async_remote_copy(
            src_ref=part_send.at[s, :, spans[kind]],
            dst_ref=part_recv.at[me, :, spans[kind]],
            send_sem=part_send_sem.at[2 * s + kind],
            recv_sem=part_recv_sem.at[2 * me + kind],
            device_id=(s, band),
            device_id_type=MESH,
        )

    def part_arrival(s, kind):
        return pltpu.make_async_remote_copy(
            src_ref=part_send.at[s, :, spans[kind]],
            dst_ref=part_recv.at[s, :, spans[kind]],
            send_sem=part_send_sem.at[2 * s + kind],
            recv_sem=part_recv_sem.at[2 * s + kind],
            device_id=(s, band),
            device_id_type=MESH,
        )

    def stage(s, sums):
        for slot, row in enumerate(order):
            part_send[s, :, slot] = sums[:, row].astype(BF16)

    for k in range(1, pairs + 1):
        pair = lax.rem(lax.div(me, 2) + k, pairs)
        total = jnp.zeros((2 * cells, chans), F32)
        for dt in range(3):
            windows = []
            for dy in range(3):
                for dx in range(3):
                    start = pair * (2 * frames) + dt
                    view = shifted[dx, pl.ds(start, 2 * frames), pl.ds(dy, rows)]
                    windows.append(view.reshape(2 * cells, LANES))
            total = total + jnp.dot(
                jnp.concatenate(windows, axis=1),
                wpad[pl.ds(dt * 9 * LANES, 9 * LANES)],
                preferred_element_type=F32,
            )
        sums = total.reshape(2, frames, rows, width, chans)
        if k < pairs:
            for c in range(2):
                stage(2 * pair + c, sums[c])
            for kind in range(2):
                for c in range(2):
                    part_copy(2 * pair + c, kind).start()
        else:
            own[...] = sums
            mate = 2 * lax.div(me, 2) + (1 - lax.rem(me, 2))
            stage(mate, own[1 - lax.rem(me, 2)])
            for kind in range(2):
                part_copy(mate, kind).start()

    load_bias1.wait()
    bias1 = bias1_ref[...].reshape(1, 1, chans)

    def finish(kind):
        for d in range(1, n_tm):
            part_arrival(lax.rem(me + n_tm - d, n_tm), kind).wait_recv()
        for slot, row in enumerate(order):
            if (slot >= 2) != (kind == 1):
                continue
            summed = own[lax.rem(me, 2), :, row] + bias1 + latent_ref[:, row].astype(F32)
            for d in range(1, n_tm):
                summed = summed + part_recv[lax.rem(me + n_tm - d, n_tm), :, slot].astype(F32)
            block[:, row + 1] = summed.astype(BF16)

    finish(0)

    def row_copy(kind, row, where, to):
        return pltpu.make_async_remote_copy(
            src_ref=block.at[:, pl.ds(row, 1)],
            dst_ref=block.at[:, pl.ds(where, 1)],
            send_sem=row_send_sem.at[kind],
            recv_sem=row_recv_sem.at[kind],
            device_id=(me, to),
            device_id_type=MESH,
        )

    @pl.when(has_below)
    def _():
        row_copy(0, rows, 0, below).start()

    @pl.when(has_above)
    def _():
        row_copy(1, 1, rows + 1, above).start()

    finish(1)
    load_wu.wait()
    load_bias2.wait()

    @pl.when(has_above)
    def _():
        row_copy(0, rows, 0, above).wait_recv()

    @pl.when(has_below)
    def _():
        row_copy(1, 1, rows + 1, below).wait_recv()

    spread = jnp.dot(
        pick[...],
        block[...].reshape(frames * depth * width, chans),
        preferred_element_type=F32,
    ).astype(BF16)
    high = frames * width * big
    lines = jnp.concatenate([spread[k * high : (k + 1) * high] for k in range(3)], axis=1)
    cols = []
    for dx in range(3):
        weights = jnp.concatenate([wu_ref[dx], wu_ref[3 + dx], wu_ref[6 + dx]], axis=1)
        product = lax.dot_general(
            lines, weights, (((1,), (1,)), ((), ())), preferred_element_type=F32
        )
        cols.append(product.reshape(width, frames * big, outputs))
    nothing = jnp.zeros((1, frames * big, outputs), F32)
    before = jnp.concatenate([nothing, cols[0][: width - 1]], axis=0)
    after = jnp.concatenate([cols[2][1:], nothing], axis=0)
    bias2 = bias2_ref[...].reshape(1, 1, outputs)
    even = before + cols[1] + cols[2] + bias2
    odd = cols[0] + cols[1] + after + bias2
    both = jnp.concatenate([even, odd], axis=-1).astype(BF16)
    for c in range(width):
        out_ref[:, pl.ds(c * 2 * outputs, 2 * outputs)] = both[c]

    for d in range(1, n_tm):
        s = lax.rem(me + d, n_tm)
        main_copy(s).wait_send()
        for kind in range(2):
            part_copy(s, kind).wait_send()

    @pl.when(has_below)
    def _():
        for s in range(n_tm):
            down_copy(s).wait_send()
        row_copy(0, rows, 0, below).wait_send()

    @pl.when(has_above)
    def _():
        for s in range(n_tm):
            up_copy(s).wait_send()
        row_copy(1, 1, rows + 1, above).wait_send()


def local(n_tm, n_rows, latent, gain_first, conv_first, bias_first, conv_upper, bias_upper):
    frames, rows, width, chans = latent.shape
    outputs = conv_upper.shape[2]
    taps, piece, _ = conv_first.shape
    cells = frames * rows * width
    all_frames = n_tm * frames
    depth = rows + 4
    vmem = pl.BlockSpec(memory_space=pltpu.VMEM)
    hbm = pl.BlockSpec(memory_space=pl.ANY)
    dma = pltpu.SemaphoreType.DMA
    flops = 2 * taps * piece * chans * all_frames * rows * width + 18 * 4 * cells * chans * outputs
    decoded = pl.pallas_call(
        functools.partial(kernel, n_tm, n_rows),
        out_shape=jax.ShapeDtypeStruct((frames * 2 * rows, 2 * width * outputs), BF16),
        in_specs=[hbm] * 6,
        out_specs=vmem,
        scratch_shapes=[
            pltpu.VMEM(latent.shape, BF16),
            pltpu.VMEM((chans,), F32),
            pltpu.VMEM((chans,), F32),
            pltpu.VMEM((outputs,), F32),
            pltpu.VMEM(conv_first.shape, BF16),
            pltpu.VMEM((taps * LANES, chans), BF16),
            pltpu.VMEM((9, outputs, chans), BF16),
            pltpu.VMEM((n_tm, frames, rows, width, LANES), BF16),
            pltpu.VMEM((all_frames, rows + 2, width, LANES), BF16),
            pltpu.VMEM((3, all_frames + 2, rows + 2, width, LANES), BF16),
            pltpu.VMEM((n_tm, frames, rows, width, chans), BF16),
            pltpu.VMEM((n_tm, frames, rows, width, chans), BF16),
            pltpu.VMEM((2, frames, rows, width, chans), F32),
            pltpu.VMEM((frames, depth, width, chans), BF16),
            pltpu.VMEM((6 * cells, frames * depth * width), BF16),
            dma((6,)),
            dma((3 * n_tm,)),
            dma((3 * n_tm,)),
            dma((2 * n_tm,)),
            dma((2 * n_tm,)),
            dma((2,)),
            dma((2,)),
        ],
        compiler_params=pltpu.CompilerParams(
            collective_id=0, has_side_effects=True, vmem_limit_bytes=60 * 1024 * 1024
        ),
        cost_estimate=pl.CostEstimate(
            flops=flops, bytes_accessed=4 * 1024 * 1024, transcendentals=cells * chans
        ),
    )(
        latent,
        gain_first,
        bias_first,
        bias_upper,
        conv_first,
        jnp.swapaxes(conv_upper, 1, 2),
    )
    return decoded.reshape(frames, 2 * rows, 2 * width * outputs)


def solution(mesh):
    in_specs = (P("tm", "rows", None, None), P(), P(None, "tm", None), P(), P(), P())
    out_specs = P("tm", "rows", None)
    body = functools.partial(local, mesh.shape["tm"], mesh.shape["rows"])
    return jax.shard_map(body, mesh=mesh, in_specs=in_specs, out_specs=out_specs, check_vma=False)
```

```python
import functools

import jax
import jax.numpy as jnp
from jax import lax
from jax.experimental import pallas as pl
from jax.experimental.pallas import tpu as pltpu
from jax.sharding import PartitionSpec as P

MESH = pl.DeviceIdType.MESH
F32 = jnp.float32
BF16 = jnp.bfloat16
LANES = 128


def quotient(number, by):
    if by & (by - 1):
        return number // by
    return lax.shift_right_logical(number, by.bit_length() - 1)


def remainder(number, by):
    return number % by if by & (by - 1) else number & (by - 1)


def kernel(
    n_tm,
    n_rows,
    latent_hbm,
    gain_hbm,
    bias1_hbm,
    bias2_hbm,
    w1_hbm,
    wu_hbm,
    out_ref,
    latent_ref,
    gain_ref,
    bias1_ref,
    bias2_ref,
    w1_ref,
    wpad,
    wu_ref,
    upper,
    send,
    recv,
    shifted,
    part_send,
    part_recv,
    own,
    block,
    pick,
    load_sem,
    act_send_sem,
    act_recv_sem,
    part_send_sem,
    part_recv_sem,
    row_send_sem,
    row_recv_sem,
):
    frames, rows, width, chans = latent_ref.shape
    cells = frames * rows * width
    taps, piece, _ = w1_ref.shape
    outputs = wu_ref.shape[1]
    me = lax.axis_index("tm")
    band = lax.axis_index("rows")
    above = lax.rem(band + n_rows - 1, n_rows)
    below = lax.rem(band + 1, n_rows)
    has_above = band > 0
    has_below = band < n_rows - 1

    load_latent = pltpu.make_async_copy(latent_hbm, latent_ref, load_sem.at[0])
    load_gain = pltpu.make_async_copy(gain_hbm, gain_ref, load_sem.at[1])
    load_w1 = pltpu.make_async_copy(w1_hbm, w1_ref, load_sem.at[2])
    load_bias1 = pltpu.make_async_copy(bias1_hbm, bias1_ref, load_sem.at[3])
    load_wu = pltpu.make_async_copy(wu_hbm, wu_ref, load_sem.at[4])
    load_bias2 = pltpu.make_async_copy(bias2_hbm, bias2_ref, load_sem.at[5])
    for load in (load_latent, load_gain, load_w1, load_bias1, load_wu, load_bias2):
        load.start()

    barrier = pltpu.get_barrier_semaphore()
    for d in range(1, n_tm):
        pl.semaphore_signal(
            barrier, inc=1, device_id=(lax.rem(me + d, n_tm), band), device_id_type=MESH
        )

    @pl.when(has_above)
    def _():
        for s in range(n_tm):
            pl.semaphore_signal(barrier, inc=1, device_id=(s, above), device_id_type=MESH)

    @pl.when(has_below)
    def _():
        for s in range(n_tm):
            pl.semaphore_signal(barrier, inc=1, device_id=(s, below), device_id_type=MESH)

    load_latent.wait()
    load_gain.wait()
    values = latent_ref[...].astype(F32).reshape(cells, chans)
    mean_square = jnp.mean(values * values, axis=-1, keepdims=True)
    scaled = values * lax.rsqrt(mean_square + 1e-06) * gain_ref[...].reshape(1, chans)
    act = scaled / (1.0 + jnp.exp(-scaled))
    blank = jnp.zeros((cells, LANES - piece), F32)
    for s in range(n_tm):
        cut = jnp.concatenate([act[:, s * piece : (s + 1) * piece], blank], axis=1)
        send[s] = cut.astype(BF16).reshape(frames, rows, width, LANES)

    neighbours = jnp.where(has_above, n_tm, 0) + jnp.where(has_below, n_tm, 0)
    pl.semaphore_wait(barrier, n_tm - 1 + neighbours)

    mine = pl.ds(me * frames, frames)

    def act_copy(s, kind, row, where, to):
        return pltpu.make_async_remote_copy(
            src_ref=send.at[s, :, row],
            dst_ref=recv.at[mine, where],
            send_sem=act_send_sem.at[3 * s + kind],
            recv_sem=act_recv_sem.at[3 * me + kind],
            device_id=(s, to),
            device_id_type=MESH,
        )

    def main_copy(s):
        return act_copy(s, 0, pl.ds(0, rows), pl.ds(1, rows), band)

    def down_copy(s):
        return act_copy(s, 1, pl.ds(rows - 1, 1), pl.ds(0, 1), below)

    def up_copy(s):
        return act_copy(s, 2, pl.ds(0, 1), pl.ds(rows + 1, 1), above)

    for d in range(1, n_tm):
        main_copy(lax.rem(me + d, n_tm)).start()

    @pl.when(has_below)
    def _():
        for s in range(n_tm):
            down_copy(s).start()

    @pl.when(has_above)
    def _():
        for s in range(n_tm):
            up_copy(s).start()

    recv[mine, pl.ds(1, rows)] = send[me]
    all_frames = n_tm * frames
    edge = jnp.zeros((all_frames, 1, width, LANES), BF16)
    block_edge = jnp.zeros((frames, 1, width, chans), BF16)

    @pl.when(band == 0)
    def _():
        recv[:, pl.ds(0, 1)] = edge
        block[:, pl.ds(0, 1)] = block_edge

    @pl.when(band == n_rows - 1)
    def _():
        recv[:, pl.ds(rows + 1, 1)] = edge
        block[:, pl.ds(rows + 1, 1)] = block_edge

    shifted[:, pl.ds(0, 2)] = jnp.zeros((3, 2, rows + 2, width, LANES), BF16)

    big = 2 * rows
    depth = block.shape[1]
    block[:, pl.ds(rows + 2, depth - rows - 2)] = jnp.zeros(
        (frames, depth - rows - 2, width, chans), BF16
    )
    at = lax.broadcasted_iota(jnp.int32, (pick.shape[0], 1), 0)
    to = lax.broadcasted_iota(jnp.int32, pick.shape, 1)
    row_tap = quotient(at, frames * width * big)
    col = remainder(quotient(at, frames * big), width)
    frame = remainder(quotient(at, big), frames)
    line = remainder(at, big)
    source = frame * (depth * width) + quotient(line + row_tap + 1, 2) * width + col
    pick[...] = jnp.where(to == source, 1.0, 0.0).astype(BF16)

    load_w1.wait()
    spare = jnp.zeros((LANES - piece, chans), BF16)
    for tap in range(taps):
        wpad[pl.ds(tap * LANES, LANES)] = jnp.concatenate([w1_ref[tap], spare], axis=0)

    def act_arrival(s, kind, row, where):
        return pltpu.make_async_remote_copy(
            src_ref=send.at[s, :, row],
            dst_ref=recv.at[pl.ds(s * frames, frames), where],
            send_sem=act_send_sem.at[3 * s + kind],
            recv_sem=act_recv_sem.at[3 * s + kind],
            device_id=(lax.rem(me + 1, n_tm), band),
            device_id_type=MESH,
        )

    for d in range(1, n_tm):
        s = lax.rem(me + d, n_tm)
        act_arrival(s, 0, pl.ds(0, rows), pl.ds(1, rows)).wait_recv()

    @pl.when(has_above)
    def _():
        for s in range(n_tm):
            act_arrival(s, 1, pl.ds(0, 1), pl.ds(0, 1)).wait_recv()

    @pl.when(has_below)
    def _():
        for s in range(n_tm):
            act_arrival(s, 2, pl.ds(0, 1), pl.ds(rows + 1, 1)).wait_recv()

    tall = all_frames * (rows + 2) * width
    flat = recv[...].astype(F32).reshape(tall, LANES)
    column = remainder(lax.broadcasted_iota(jnp.int32, (tall, LANES), 0), width)
    left = jnp.where(column == 0, 0.0, pltpu.roll(flat, 1, 0))
    right = jnp.where(column == width - 1, 0.0, pltpu.roll(flat, tall - 1, 0))
    shape = (all_frames, rows + 2, width, LANES)
    shifted[0, pl.ds(2, all_frames)] = left.astype(BF16).reshape(shape)
    shifted[1, pl.ds(2, all_frames)] = recv[...]
    shifted[2, pl.ds(2, all_frames)] = right.astype(BF16).reshape(shape)

    pairs = n_tm // 2

    order = [0, rows - 1] + list(range(1, rows - 1))
    spans = (pl.ds(0, 2), pl.ds(2, rows - 2))

    def part_copy(s, kind):
        return pltpu.make_async_remote_copy(
            src_ref=part_send.at[s, :, spans[kind]],
            dst_ref=part_recv.at[me, :, spans[kind]],
            send_sem=part_send_sem.at[2 * s + kind],
            recv_sem=part_recv_sem.at[2 * me + kind],
            device_id=(s, band),
            device_id_type=MESH,
        )

    def part_arrival(s, kind):
        return pltpu.make_async_remote_copy(
            src_ref=part_send.at[s, :, spans[kind]],
            dst_ref=part_recv.at[s, :, spans[kind]],
            send_sem=part_send_sem.at[2 * s + kind],
            recv_sem=part_recv_sem.at[2 * s + kind],
            device_id=(s, band),
            device_id_type=MESH,
        )

    def stage(s, sums):
        for slot, row in enumerate(order):
            part_send[s, :, slot] = sums[:, row].astype(BF16)

    for k in range(1, pairs + 1):
        pair = lax.rem(lax.div(me, 2) + k, pairs)
        windows = []
        for dt in range(3):
            for dy in range(3):
                for dx in range(3):
                    start = pair * (2 * frames) + dt
                    view = shifted[dx, pl.ds(start, 2 * frames), pl.ds(dy, rows)]
                    windows.append(view.reshape(2 * cells, LANES))
        total = jnp.dot(
            jnp.concatenate(windows, axis=1), wpad[...], preferred_element_type=F32
        )
        sums = total.reshape(2, frames, rows, width, chans)
        if k < pairs:
            for c in range(2):
                stage(2 * pair + c, sums[c])
            for kind in range(2):
                for c in range(2):
                    part_copy(2 * pair + c, kind).start()
        else:
            own[...] = sums
            mate = 2 * lax.div(me, 2) + (1 - lax.rem(me, 2))
            stage(mate, own[1 - lax.rem(me, 2)])
            for kind in range(2):
                part_copy(mate, kind).start()

    load_wu.wait()
    for dx in range(3):
        taken = jnp.concatenate([wu_ref[dx], wu_ref[3 + dx], wu_ref[6 + dx]], axis=1)
        upper[dx] = taken.T

    load_bias1.wait()
    bias1 = bias1_ref[...].reshape(1, 1, chans)

    def finish(kind):
        for d in range(1, n_tm):
            part_arrival(lax.rem(me + n_tm - d, n_tm), kind).wait_recv()
        for slot, row in enumerate(order):
            if (slot >= 2) != (kind == 1):
                continue
            summed = own[lax.rem(me, 2), :, row] + bias1 + latent_ref[:, row].astype(F32)
            for d in range(1, n_tm):
                summed = summed + part_recv[lax.rem(me + n_tm - d, n_tm), :, slot].astype(F32)
            block[:, row + 1] = summed.astype(BF16)

    finish(0)

    def row_copy(kind, row, where, to):
        return pltpu.make_async_remote_copy(
            src_ref=block.at[:, pl.ds(row, 1)],
            dst_ref=block.at[:, pl.ds(where, 1)],
            send_sem=row_send_sem.at[kind],
            recv_sem=row_recv_sem.at[kind],
            device_id=(me, to),
            device_id_type=MESH,
        )

    @pl.when(has_below)
    def _():
        row_copy(0, rows, 0, below).start()

    @pl.when(has_above)
    def _():
        row_copy(1, 1, rows + 1, above).start()

    finish(1)
    load_bias2.wait()

    @pl.when(has_above)
    def _():
        row_copy(0, rows, 0, above).wait_recv()

    @pl.when(has_below)
    def _():
        row_copy(1, 1, rows + 1, below).wait_recv()

    spread = jnp.dot(
        pick[...],
        block[...].reshape(frames * depth * width, chans),
        preferred_element_type=F32,
    ).astype(BF16)
    high = frames * width * big
    lines = jnp.concatenate([spread[k * high : (k + 1) * high] for k in range(3)], axis=1)
    cols = []
    for dx in range(3):
        product = jnp.dot(lines, upper[dx], preferred_element_type=F32)
        cols.append(product.reshape(width, frames * big, outputs))
    nothing = jnp.zeros((1, frames * big, outputs), F32)
    before = jnp.concatenate([nothing, cols[0][: width - 1]], axis=0)
    after = jnp.concatenate([cols[2][1:], nothing], axis=0)
    bias2 = bias2_ref[...].reshape(1, 1, outputs)
    even = before + cols[1] + cols[2] + bias2
    odd = cols[0] + cols[1] + after + bias2
    both = jnp.concatenate([even, odd], axis=-1).astype(BF16)
    for c in range(width):
        out_ref[:, pl.ds(c * 2 * outputs, 2 * outputs)] = both[c]

    for d in range(1, n_tm):
        s = lax.rem(me + d, n_tm)
        main_copy(s).wait_send()
        for kind in range(2):
            part_copy(s, kind).wait_send()

    @pl.when(has_below)
    def _():
        for s in range(n_tm):
            down_copy(s).wait_send()
        row_copy(0, rows, 0, below).wait_send()

    @pl.when(has_above)
    def _():
        for s in range(n_tm):
            up_copy(s).wait_send()
        row_copy(1, 1, rows + 1, above).wait_send()


def local(n_tm, n_rows, latent, gain_first, conv_first, bias_first, conv_upper, bias_upper):
    frames, rows, width, chans = latent.shape
    outputs = conv_upper.shape[2]
    taps, piece, _ = conv_first.shape
    cells = frames * rows * width
    all_frames = n_tm * frames
    depth = rows + 4
    vmem = pl.BlockSpec(memory_space=pltpu.VMEM)
    hbm = pl.BlockSpec(memory_space=pl.ANY)
    dma = pltpu.SemaphoreType.DMA
    flops = 2 * taps * piece * chans * all_frames * rows * width + 18 * 4 * cells * chans * outputs
    decoded = pl.pallas_call(
        functools.partial(kernel, n_tm, n_rows),
        out_shape=jax.ShapeDtypeStruct((frames * 2 * rows, 2 * width * outputs), BF16),
        in_specs=[hbm] * 6,
        out_specs=vmem,
        scratch_shapes=[
            pltpu.VMEM(latent.shape, BF16),
            pltpu.VMEM((chans,), F32),
            pltpu.VMEM((chans,), F32),
            pltpu.VMEM((outputs,), F32),
            pltpu.VMEM(conv_first.shape, BF16),
            pltpu.VMEM((taps * LANES, chans), BF16),
            pltpu.VMEM((9, outputs, chans), BF16),
            pltpu.VMEM((3, 3 * chans, outputs), BF16),
            pltpu.VMEM((n_tm, frames, rows, width, LANES), BF16),
            pltpu.VMEM((all_frames, rows + 2, width, LANES), BF16),
            pltpu.VMEM((3, all_frames + 2, rows + 2, width, LANES), BF16),
            pltpu.VMEM((n_tm, frames, rows, width, chans), BF16),
            pltpu.VMEM((n_tm, frames, rows, width, chans), BF16),
            pltpu.VMEM((2, frames, rows, width, chans), F32),
            pltpu.VMEM((frames, depth, width, chans), BF16),
            pltpu.VMEM((6 * cells, frames * depth * width), BF16),
            dma((6,)),
            dma((3 * n_tm,)),
            dma((3 * n_tm,)),
            dma((2 * n_tm,)),
            dma((2 * n_tm,)),
            dma((2,)),
            dma((2,)),
        ],
        compiler_params=pltpu.CompilerParams(
            collective_id=0, has_side_effects=True, vmem_limit_bytes=60 * 1024 * 1024
        ),
        cost_estimate=pl.CostEstimate(
            flops=flops, bytes_accessed=4 * 1024 * 1024, transcendentals=cells * chans
        ),
    )(
        latent,
        gain_first,
        bias_first,
        bias_upper,
        conv_first,
        jnp.swapaxes(conv_upper, 1, 2),
    )
    return decoded.reshape(frames, 2 * rows, 2 * width * outputs)


def solution(mesh):
    in_specs = (P("tm", "rows", None, None), P(), P(None, "tm", None), P(), P(), P())
    out_specs = P("tm", "rows", None)
    body = functools.partial(local, mesh.shape["tm"], mesh.shape["rows"])
    return jax.shard_map(body, mesh=mesh, in_specs=in_specs, out_specs=out_specs, check_vma=False)
```
